32 devices in a mesh: groups: 2 (over y), tile: 8 (over z, x), col: 2 (over core).
Axes of the slice: x: 2, y: 2, z: 4, core: 2. Of those that a mesh axis runs over, the one named last changes fastest.
Arguments:
- jacobian: bfloat16 [512, 3, 128, 512], P(('groups', 'tile'), None, None, 'col'), parts along dimension 0, may hold values from -0.15625 to 0.15625
- footprint: int32 [512, 3], P(('groups', 'tile')), parts along dimension 0, may hold values from 0 to 4, all different within a row
- live: int32 [16], P(('groups', 'tile')), parts along dimension 0, may hold values from 1 to 32, as said below
- noise_weight: float32 [512, 128], P(('groups', 'tile')), parts along dimension 0, may hold values from 0.25 to 4
- probes: bfloat16 [16, 512, 256], P(('groups', 'tile'), 'col'), parts along dimension 0, may hold values from -6 to 6
Outputs:
- basis: float32 [16, 512, 256], P(('groups', 'tile'), 'col'), parts along dimension 0
- factor: float32 [512, 256], P('groups'), parts along dimension 0
The draws below stay inside these ranges and needn't reach their ends.
There are 2 independent parts, one for each index of `groups`. The reference program is written for one: setup_inputs(seed, part) draws one part's arguments, and reference() takes and returns one part's arrays. A program takes and returns all parts, laid end to end along the dimension named above; each array names one. Nothing has to cross between parts.
Inputs may be any that keep to these rules, and one draw needn't show every extreme that they name: `footprint`: each row lists 3 different offsets. Some band has all 32 slots live.
All inputs are finite; a program needn't handle non-finite values.
Results may differ from the reference program's by a relative error of at most 0.0014.
Values may be sent and summed in bfloat16 or wider, within the bound.
No kernel may reach another device: no remote copies, remote signals or barrier semaphores. Data moves between devices by JAX's collectives and lax.ppermute only.
A program may use at most 64 MiB of HBM per device.

```python
import math
import jax
import jax.numpy as jnp
from jax import lax

PROBES = 256
TOUCHED = 3
BLOCK_ROWS = 128
SLOTS = 32
BANDS = 8
TILE_CELLS = 512
BLOCKS = 256


def draw_live(key, part):
    counts = jax.random.randint(key, (BANDS,), 1, SLOTS + 1)
    where = jax.random.randint(jax.random.fold_in(key, 7), (), 0, BANDS)
    return counts.at[where].set(SLOTS).astype(jnp.int32)


def block_levels(own_key, extent, split, low, high):
    def one(dim, parts):
        steps = jax.random.uniform(jax.random.fold_in(jax.random.fold_in(own_key, 6), dim), (parts,), jnp.float32, low / len(split), high / len(split))
        return jnp.repeat(jnp.exp(steps), extent[dim] // parts).reshape((-1,) + (1,) * (len(extent) - dim - 1))

    factor_of = one(*split[0])
    for cut in split[1:]:
        factor_of = factor_of * one(*cut)
    return factor_of


def different_ones(own_key, rows, number_of, top, lift):
    ranking = jax.random.permutation(jax.random.fold_in(own_key, 1), number_of)
    boost = ranking
    for power in range(3):
        boost = boost * boost // number_of
    boost = boost * lift // number_of
    lots = jax.random.randint(jax.random.fold_in(own_key, 2), (rows, number_of), 0, 4096) + boost
    sure = jax.random.permutation(jax.random.fold_in(own_key, 3), rows)[jnp.arange(number_of) % rows]
    lots = jnp.where(jnp.arange(rows)[:, None] == sure[None, :], 1 << 14, lots)
    merit = lots * number_of + jnp.arange(number_of)
    return lax.top_k(merit.astype(jnp.int32), top)[1].astype(jnp.int32)


def centred(own_key, dims, scale, reach, shards=(), kind=jnp.bfloat16):
    loudness = block_levels(own_key, dims, shards, -0.22, 0.18) if shards else 1.0
    array = jax.random.normal(own_key, dims, jnp.float32) * scale * loudness
    return jnp.minimum(jnp.maximum(array, -reach), reach).astype(kind)


def setup_inputs(seed: int = 0, part: int = 0) -> dict:
    streams_of = jax.random.split(jax.random.key(seed), 6)
    part_keys = jax.random.split(jax.random.fold_in(streams_of[5], part), 6)
    return {
        "jacobian": centred(part_keys[0], (BLOCKS, TOUCHED, BLOCK_ROWS, TILE_CELLS), (TOUCHED * TILE_CELLS) ** -0.5, 0.15625, ((0, 8), (3, 2))),
        "footprint": different_ones(part_keys[1], BLOCKS, 5, TOUCHED, 0),
        "live": draw_live(jax.random.fold_in(jax.random.fold_in(streams_of[5], part), 71), part),
        "noise_weight": jnp.clip(jnp.exp(math.log(4.0) - 2.7725887 * jax.random.uniform(part_keys[3], (BLOCKS, BLOCK_ROWS), jnp.float32) ** block_levels(part_keys[3], (BLOCKS, BLOCK_ROWS), ((0, 8),), -0.2, 0.2)), 0.25, 4.0),
        "probes": centred(part_keys[4], (BANDS, TILE_CELLS, PROBES), 1.0, 6.0, ((0, 8), (1, 2))),
    }


def reference(jacobian, footprint, live, noise_weight, probes):
    bands, tile_cells, width = probes.shape
    blocks_all = jacobian.reshape(bands, SLOTS, TOUCHED, BLOCK_ROWS, tile_cells)
    foot_all = footprint.reshape(bands, SLOTS, TOUCHED)
    weight_all = noise_weight.reshape(bands, SLOTS, BLOCK_ROWS)
    probe_full = probes.astype(jnp.float32)
    offsets = jnp.arange(5, dtype=jnp.int32) - 2

    def band_step(total, band):
        foot_here = foot_all[band]
        tiles = (band + foot_here - 2) % bands
        picked = probe_full[tiles]
        block = blocks_all[band].astype(jnp.float32)
        images = jnp.einsum('sfrc,sfck->srk', block, picked)
        active = (jnp.arange(SLOTS, dtype=jnp.int32) < live[band]).astype(jnp.float32)
        scaling = weight_all[band] * active[:, None]
        weighted = (images * scaling[:, :, None]).astype(jnp.bfloat16)
        weighted = lax.optimization_barrier(weighted).astype(jnp.float32)
        contrib = jnp.einsum('sfrc,srk->sfck', block, weighted)
        onehot = (foot_here[:, :, None] == jnp.arange(5, dtype=jnp.int32)[None, None, :]).astype(jnp.float32)
        bucket = jnp.einsum('sfo,sfck->ock', onehot, contrib, precision=lax.Precision.HIGHEST)
        return (total.at[(band + offsets) % bands].add(bucket), None)
    total, _ = lax.scan(band_step, jnp.zeros_like(probe_full), jnp.arange(bands, dtype=jnp.int32))
    sketch = (probe_full + total).reshape(bands * tile_cells, width)
    gram = jnp.dot(sketch.T, sketch, precision=lax.Precision.HIGHEST)
    lower = jnp.linalg.cholesky(gram)
    scale = jnp.sqrt(jnp.float32(bands * tile_cells))
    solved = jax.scipy.linalg.solve_triangular(lower, sketch.T, lower=True)
    basis = (solved.T * scale).reshape(bands, tile_cells, width)
    factor = lower.T / scale
    return (basis, factor)
```

```python
import functools
import math

import jax
import jax.numpy as jnp
from jax import lax
from jax.experimental import pallas as pl
from jax.experimental.pallas import tpu as pltpu
from jax.sharding import PartitionSpec as P

F32 = jnp.float32
BF16 = jnp.bfloat16
NN = (((1,), (0,)), ((), ()))
NT = (((1,), (1,)), ((), ()))
OFFSETS = (-2, -1, 0, 1, 2)
PAD = 16
LIMIT = 48 << 20
VMEM = pl.BlockSpec(memory_space=pltpu.VMEM)
SMEM = pl.BlockSpec(memory_space=pltpu.SMEM)
FWD_GROUP = 4
BWD_GROUP = 4
MAX_GROUP = 8


def kernel_call(body, out_shape, in_specs, out_specs, scratch=(), flops=0, nbytes=0):
    return pl.pallas_call(
        body,
        out_shape=out_shape,
        in_specs=in_specs,
        out_specs=out_specs,
        scratch_shapes=list(scratch),
        compiler_params=pltpu.CompilerParams(vmem_limit_bytes=LIMIT),
        cost_estimate=pl.CostEstimate(flops=flops, bytes_accessed=nbytes, transcendentals=0),
    )


def dot(a, b, dims=NN):
    return lax.dot_general(a, b, dims, preferred_element_type=F32)


def halves(a):
    high = a.astype(BF16)
    return high, (a - high.astype(F32)).astype(BF16)


def dot3(a, b, dims=NN):
    a_high, a_low = a
    b_high, b_low = b
    return dot(a_high, b_high, dims) + (dot(a_high, b_low, dims) + dot(a_low, b_high, dims))


def shifted(value, axis, steps):
    count = lax.axis_size(axis)
    pairs = [(source, (source + steps) % count) for source in range(count)]
    return lax.ppermute(value, axis, pairs)


def flipped(value):
    return shifted(value, "col", 1)


def list_kernel(cap, half, footprint, live, core, ids, own, every):
    slots, reach = footprint.shape
    for o in range(len(OFFSETS)):
        every[o] = 0

    def step(j, _):
        slot = lax.rem(j + core[0] * half, slots)
        alive = (slot < live[0]).astype(jnp.int32)
        for f in range(reach):
            o = footprint[slot, f]
            n = every[o]
            ids[o * cap + n] = j * 4 + f
            every[o] = n + alive
        return 0

    lax.fori_loop(0, half, step, 0)
    for o in range(len(OFFSETS)):
        own[o] = every[o]
    lax.fori_loop(half, slots, step, 0)


def forward_kernel(cap, ids, own, core, jac_near, jac_far, *rest):
    near, far = rest[:5], rest[5:10]
    noise, out, window, images = rest[10:]
    half, _, rows, cells = jac_near.shape
    for o in range(len(OFFSETS)):
        window[o, :cells] = near[o][...]
        window[o, cells:] = far[o][...]

    def clear(j, _):
        images[j] = jnp.zeros(images.shape[1:], F32)
        return 0

    lax.fori_loop(0, half, clear, 0)
    for o in range(len(OFFSETS)):
        count = own[o]

        def step(i, _):
            slots, parts = [], []
            for q in range(FWD_GROUP):
                n = i * FWD_GROUP + q
                code = jnp.where(n < count, ids[o * cap + n], half * 4)
                j, f = lax.div(code, 4), lax.rem(code, 4)
                slots.append(j)
                jj = jnp.minimum(j, half - 1)
                parts.append(jnp.concatenate([jac_near[jj, f], jac_far[jj, f]], axis=1))
            product = dot(jnp.concatenate(parts, axis=0), window[o])
            for q in range(FWD_GROUP):
                images[slots[q]] += product[q * rows : (q + 1) * rows]
            return 0

        lax.fori_loop(0, lax.div(count + FWD_GROUP - 1, FWD_GROUP), step, 0)

    def finish(j, _):
        scale = noise[pl.ds(core[0] * half + j, 1), :]
        out[j] = (images[j].T * scale).astype(BF16)
        return 0

    lax.fori_loop(0, half, finish, 0)


def gather_kernel(mine, other, out):
    half = mine.shape[0]

    def step(j, _):
        out[j] = mine[j]
        out[half + j] = other[j]
        return 0

    lax.fori_loop(0, half, step, 0)
    out[2 * half] = jnp.zeros(out.shape[1:], BF16)


def backward_kernel(o, cap, ids, every, jac, weighted, out, total):
    slots = jac.shape[0]
    width = weighted.shape[1]
    count = every[o]
    total[...] = jnp.zeros_like(total)

    def step(i, _):
        left, right = [], []
        for q in range(BWD_GROUP):
            n = i * BWD_GROUP + q
            code = jnp.where(n < count, ids[o * cap + n], slots * 4)
            j, f = lax.div(code, 4), lax.rem(code, 4)
            left.append(weighted[j])
            right.append(jac[jnp.minimum(j, slots - 1), f])
        total[...] += dot(jnp.concatenate(left, axis=1), jnp.concatenate(right, axis=0))
        return 0

    lax.fori_loop(0, lax.div(count + BWD_GROUP - 1, BWD_GROUP), step, 0)
    value = total[...]
    if OFFSETS[o] == 0:
        out[...] = value
        return
    top = jnp.max(jnp.abs(value), axis=0, keepdims=True)
    power = jnp.clip(jnp.floor(jnp.log2(jnp.maximum(top, 1e-30))) + 1.0, -96.0, 96.0)
    coded = jnp.clip(jnp.round(value * jnp.exp2(15.0 - power)), -32767.0, 32767.0)
    out[:width] = coded.astype(jnp.int32).astype(jnp.int16)
    rows = jnp.broadcast_to(power.astype(jnp.int32), (PAD, power.shape[1]))
    out[width:] = rows.astype(jnp.int16)


def field_kernel(core, probes, own, *rest):
    parts, (field, keep, send) = rest[:4], rest[4:]
    width = own.shape[0]
    total = probes[...].astype(F32).T + own[...]
    for part in parts:
        power = part[width:].astype(jnp.int32).astype(F32)[:1]
        total = total + part[:width].astype(jnp.int32).astype(F32) * jnp.exp2(power - 15.0)
    field[...] = total
    both = halves(total)
    gram = dot3(both, both, NT)
    mid, quarter = width // 2, width // 4
    lower = [gram[:mid, :mid], gram[mid : mid + quarter, :mid]]
    upper = [gram[mid:, mid:], gram[mid + quarter :, :mid]]
    first = core[0] == 0
    low, high = jnp.concatenate(lower, axis=0), jnp.concatenate(upper, axis=0)
    keep[...] = jnp.where(first, low, high)
    send[...] = jnp.where(first, high, low)


def finish_kernel(scale, rounds, core, mine, other, field, basis, factor, gram, inverse, a_high, a_low):
    width = gram.shape[0]
    mid, quarter = width // 2, width // 4
    first = core[0] == 0
    low = jnp.where(first, mine[...], other[...])
    high = jnp.where(first, other[...], mine[...])
    corner = jnp.concatenate([low[mid:], high[mid:]], axis=0)
    gram[:mid, :mid] = low[:mid]
    gram[mid:, mid:] = high[:mid]
    gram[mid:, :mid] = corner
    gram[:mid, mid:] = corner.T
    matrix = gram[...]
    row = lax.broadcasted_iota(jnp.int32, matrix.shape, 0)
    column = lax.broadcasted_iota(jnp.int32, matrix.shape, 1)
    eye = (row == column).astype(F32)
    diagonal = matrix * eye
    down = lax.rsqrt(jnp.sum(diagonal, axis=1, keepdims=True))
    along = lax.rsqrt(jnp.sum(diagonal, axis=0, keepdims=True))
    unit = matrix * down * along
    parts = halves(unit)
    a_high[...], a_low[...] = parts

    def correction(error):
        return jnp.where(row > column, error, 0.5 * eye * error).astype(BF16)

    now = (eye - jnp.where(row > column, unit, 0.0)).astype(BF16)
    for _ in range(rounds):
        error = dot(dot(now, a_high[...]).astype(BF16), now, NT) - eye
        now = (now.astype(F32) - dot(correction(error), now)).astype(BF16)
    exact = now.astype(F32)
    applied = dot(now, a_high[...]) + dot(now, a_low[...])
    applied_high, applied_low = halves(applied)
    error = dot(applied_high, now, NT) + dot(applied_low, now, NT) - eye
    exact = exact - dot(correction(error), now)
    full = halves(exact)
    error = dot3(halves(dot3(full, (a_high[...], a_low[...]))), full, NT) - eye
    inverse[...] = (exact - dot(correction(error), full[0])) * along
    left = jnp.sum(error * error)

    @pl.when(jnp.logical_not(left < 1e-4))
    def _():
        inverse[...] = eye
        across = lax.broadcasted_iota(jnp.int32, (1, width), 1)
        down_at = lax.broadcasted_iota(jnp.int32, (width, 1), 0)

        def eliminate(k, _):
            pivot_row = gram[pl.ds(k, 1), :]
            pivot = jnp.sum(jnp.where(across == k, pivot_row, 0.0), axis=1, keepdims=True)
            scaled = pivot_row * lax.rsqrt(pivot)
            now = gram[...]
            below = jnp.sum(jnp.where(column == k, now, 0.0), axis=1, keepdims=True)
            below = jnp.where(down_at > k, below * lax.rsqrt(pivot), 0.0)
            done = inverse[pl.ds(k, 1), :] * lax.rsqrt(pivot)
            gram[...] = now - below * scaled
            inverse[...] = inverse[...] - below * done
            inverse[pl.ds(k, 1), :] = done
            return 0

        lax.fori_loop(0, width, eliminate, 0)

    solved = halves(inverse[...])
    upper = dot3(solved, halves(matrix)) * (1.0 / scale)
    factor[...] = jnp.where(row <= column, upper, 0.0)
    basis[...] = (dot3(solved, halves(field[...])) * scale).T


def all_reduced(value):
    count = lax.axis_size("tile")
    if count & (count - 1):
        return lax.psum(value, "tile")
    mask = 1
    while mask < count:
        jump = mask if mask < 4 else mask + mask // 2
        value = value + lax.ppermute(value, "tile", [(i, i ^ jump) for i in range(count)])
        mask *= 2
    return value


def on_device(jacobian, footprint, live, noise_weight, probes):
    slots, reach, rows, cells = jacobian.shape
    width = probes.shape[2]
    half = slots // lax.axis_size("col")
    cap = slots + MAX_GROUP
    core = lax.axis_index("col").astype(jnp.int32).reshape(1)
    mine = probes[0]

    near = [mine if offset == 0 else shifted(mine, "tile", -offset) for offset in OFFSETS]
    far = [flipped(piece) for piece in near]
    start = core[0] * half
    own_share = lax.dynamic_slice_in_dim(jacobian, start, half, 0)
    other_share = lax.dynamic_slice_in_dim(jacobian, half - start, half, 0)
    jac_far = flipped(other_share)
    jac_all = jnp.concatenate([own_share, other_share], axis=0)

    def smem(n):
        return jax.ShapeDtypeStruct((n,), jnp.int32)

    ids, own, every = kernel_call(
        functools.partial(list_kernel, cap, half),
        (smem(len(OFFSETS) * cap), smem(len(OFFSETS)), smem(len(OFFSETS))),
        [SMEM] * 3,
        (SMEM,) * 3,
    )(footprint, live, core)

    share = 2 * half * reach * rows * 2 * cells * width
    weighted = kernel_call(
        functools.partial(forward_kernel, cap),
        jax.ShapeDtypeStruct((half, width, rows), BF16),
        [SMEM] * 3 + [VMEM] * 13,
        VMEM,
        [pltpu.VMEM((len(OFFSETS), 2 * cells, width), BF16), pltpu.VMEM((half + 1, rows, width), F32)],
        flops=share,
    )(ids, own, core, own_share, jac_far, *near, *far, noise_weight)
    weighted = kernel_call(
        gather_kernel,
        jax.ShapeDtypeStruct((2 * half + 1, width, rows), BF16),
        [VMEM] * 2,
        VMEM,
    )(weighted, flipped(weighted))

    def bucket(o):
        if OFFSETS[o] == 0:
            shape = jax.ShapeDtypeStruct((width, cells), F32)
        else:
            shape = jax.ShapeDtypeStruct((width + PAD, cells), jnp.int16)
        return kernel_call(
            functools.partial(backward_kernel, o, cap),
            shape,
            [SMEM] * 2 + [VMEM] * 2,
            VMEM,
            [pltpu.VMEM((width, cells), F32)],
            flops=share // len(OFFSETS),
        )(ids, every, jac_all, weighted)

    arrived = [shifted(bucket(o), "tile", OFFSETS[o]) for o in (0, 4, 1, 3)]
    packed = jax.ShapeDtypeStruct((3 * width // 4, width // 2), F32)
    field, keep, send = kernel_call(
        field_kernel,
        (jax.ShapeDtypeStruct((width, cells), F32), packed, packed),
        [SMEM] + [VMEM] * 6,
        (VMEM,) * 3,
    )(core, mine, bucket(2), *arrived)
    summed = all_reduced(keep + flipped(send))
    scale = math.sqrt(cells * lax.axis_size("col") * lax.axis_size("tile"))
    square = jax.ShapeDtypeStruct((width, width), F32)
    basis, factor = kernel_call(
        functools.partial(finish_kernel, scale, 2),
        (jax.ShapeDtypeStruct((cells, width), F32), square),
        [SMEM] + [VMEM] * 3,
        (VMEM,) * 2,
        [pltpu.VMEM((width, width), F32)] * 2 + [pltpu.VMEM((width, width), BF16)] * 2,
    )(core, summed, flipped(summed), field)
    return (basis[None], factor)


def solution(mesh):
    placed = (
        P(("groups", "tile"), None, None, "col"),
        P(("groups", "tile"), None),
        P(("groups", "tile")),
        P(("groups", "tile"), None),
        P(("groups", "tile"), "col", None),
    )
    return jax.shard_map(
        on_device,
        mesh=mesh,
        in_specs=placed,
        out_specs=(P(("groups", "tile"), "col", None), P("groups", None)),
        check_vma=False,
    )
```

```python
import functools
import math

import jax
import jax.numpy as jnp
from jax import lax
from jax.experimental import pallas as pl
from jax.experimental.pallas import tpu as pltpu
from jax.sharding import PartitionSpec as P

F32 = jnp.float32
BF16 = jnp.bfloat16
NN = (((1,), (0,)), ((), ()))
NT = (((1,), (1,)), ((), ()))
OFFSETS = (-2, -1, 0, 1, 2)
PAD = 16
LIMIT = 24 << 20
VMEM = pl.BlockSpec(memory_space=pltpu.VMEM)
SMEM = pl.BlockSpec(memory_space=pltpu.SMEM)
FWD_GROUP = 4
BWD_GROUP = 4
MAX_GROUP = 8


def kernel_call(body, out_shape, in_specs, out_specs, scratch=(), flops=0, nbytes=0):
    return pl.pallas_call(
        body,
        out_shape=out_shape,
        in_specs=in_specs,
        out_specs=out_specs,
        scratch_shapes=list(scratch),
        compiler_params=pltpu.CompilerParams(vmem_limit_bytes=LIMIT),
        cost_estimate=pl.CostEstimate(flops=flops, bytes_accessed=nbytes, transcendentals=0),
    )


def dot(a, b, dims=NN):
    return lax.dot_general(a, b, dims, preferred_element_type=F32)


def halves(a):
    high = a.astype(BF16)
    return high, (a - high.astype(F32)).astype(BF16)


def dot3(a, b, dims=NN):
    a_high, a_low = a
    b_high, b_low = b
    return dot(a_high, b_high, dims) + (dot(a_high, b_low, dims) + dot(a_low, b_high, dims))


def shifted(value, axis, steps):
    count = lax.axis_size(axis)
    pairs = [(source, (source + steps) % count) for source in range(count)]
    return lax.ppermute(value, axis, pairs)


def flipped(value):
    return shifted(value, "col", 1)


def swapped(value):
    return lax.ppermute(value, "tile", [(i, i ^ 1) for i in range(lax.axis_size("tile"))])


def spread(value, steps):
    count = lax.axis_size("tile")
    return lax.ppermute(value, "tile", [(i, (i + (steps, -steps)[i % 2]) % count) for i in range(count)])


ROLES = ("own", "back", "ahead", "partner", "beyond")


def place_of(role, parity):
    return {
        "own": 2,
        "back": 4 - 4 * parity,
        "ahead": 4 * parity,
        "partner": 3 - 2 * parity,
        "beyond": 1 + 2 * parity,
    }[role]


def list_kernel(cap, half, footprint, live, core, ids, own, every):
    slots, reach = footprint.shape
    for o in range(len(OFFSETS)):
        every[o] = 0

    def step(j, _):
        slot = lax.rem(j + core[0] * half, slots)
        alive = (slot < live[0]).astype(jnp.int32)
        for f in range(reach):
            o = footprint[slot, f]
            n = every[o]
            ids[o * cap + n] = j * 4 + f
            every[o] = n + alive
        return 0

    lax.fori_loop(0, half, step, 0)
    for o in range(len(OFFSETS)):
        own[o] = every[o]
    lax.fori_loop(half, slots, step, 0)


def forward_kernel(cap, ids, own, core, jac_near, jac_far, *rest):
    near, far = rest[:5], rest[5:10]
    noise, out, window, images = rest[10:]
    half = out.shape[0]
    _, _, rows, cells = jac_near.shape
    base = core[0] * half
    for i, role in enumerate(ROLES):
        o = place_of(role, core[1])
        window[o, :cells] = near[i][...]
        window[o, cells:] = far[i][...]

    def clear(j, _):
        images[j] = jnp.zeros(images.shape[1:], F32)
        return 0

    lax.fori_loop(0, half, clear, 0)
    for o in range(len(OFFSETS)):
        count = own[o]

        def step(i, _):
            slots, parts = [], []
            for q in range(FWD_GROUP):
                n = i * FWD_GROUP + q
                code = jnp.where(n < count, ids[o * cap + n], half * 4)
                j, f = lax.div(code, 4), lax.rem(code, 4)
                slots.append(j)
                jj = base + jnp.minimum(j, half - 1)
                parts.append(jnp.concatenate([jac_near[jj, f], jac_far[jj, f]], axis=1))
            product = dot(jnp.concatenate(parts, axis=0), window[o])
            for q in range(FWD_GROUP):
                images[slots[q]] += product[q * rows : (q + 1) * rows]
            return 0

        lax.fori_loop(0, lax.div(count + FWD_GROUP - 1, FWD_GROUP), step, 0)

    def finish(j, _):
        scale = noise[pl.ds(base + j, 1), :]
        out[j] = (images[j].T * scale).astype(BF16)
        return 0

    lax.fori_loop(0, half, finish, 0)


def gather_kernel(mine, other, out):
    half = mine.shape[0]

    def step(j, _):
        out[j] = mine[j]
        out[half + j] = other[j]
        return 0

    lax.fori_loop(0, half, step, 0)
    out[2 * half] = jnp.zeros(out.shape[1:], BF16)


def encode(value, out):
    width = value.shape[0]
    top = jnp.max(jnp.abs(value), axis=0, keepdims=True)
    power = jnp.clip(jnp.floor(jnp.log2(jnp.maximum(top, 1e-30))) + 1.0, -96.0, 96.0)
    coded = jnp.clip(jnp.round(value * jnp.exp2(15.0 - power)), -32767.0, 32767.0)
    out[:width] = coded.astype(jnp.int32).astype(jnp.int16)
    rows = jnp.broadcast_to(power.astype(jnp.int32), (PAD, power.shape[1]))
    out[width:] = rows.astype(jnp.int16)


def decode(part):
    width = part.shape[0] - PAD
    power = part[width:].astype(jnp.int32).astype(F32)[:1]
    return part[:width].astype(jnp.int32).astype(F32) * jnp.exp2(power - 15.0)


def backward_kernel(role, coded, cap, ids, every, core, jac, weighted, out, total):
    slots = jac.shape[0]
    half = slots // 2
    o = place_of(role, core[1])
    count = every[o]
    total[...] = jnp.zeros_like(total)

    def step(i, _):
        left, right = [], []
        for q in range(BWD_GROUP):
            n = i * BWD_GROUP + q
            code = jnp.where(n < count, ids[o * cap + n], slots * 4)
            j, f = lax.div(code, 4), lax.rem(code, 4)
            left.append(weighted[j])
            right.append(jac[lax.rem(j + core[0] * half, slots), f])
        total[...] += dot(jnp.concatenate(left, axis=1), jnp.concatenate(right, axis=0))
        return 0

    lax.fori_loop(0, lax.div(count + BWD_GROUP - 1, BWD_GROUP), step, 0)
    if coded:
        encode(total[...], out)
    else:
        out[...] = total[...]


def merge_kernel(value, part, out):
    encode(value[...] + decode(part), out)


def field_kernel(core, probes, own, *rest):
    parts, (field, keep, send) = rest[:3], rest[3:]
    width = own.shape[0]
    total = probes[...].astype(F32).T + own[...]
    for part in parts:
        total = total + decode(part)
    field[...] = total
    both = halves(total)
    gram = dot3(both, both, NT)
    mid, quarter = width // 2, width // 4
    lower = [gram[:mid, :mid], gram[mid : mid + quarter, :mid]]
    upper = [gram[mid:, mid:], gram[mid + quarter :, :mid]]
    first = core[0] == 0
    low, high = jnp.concatenate(lower, axis=0), jnp.concatenate(upper, axis=0)
    keep[...] = jnp.where(first, low, high)
    send[...] = jnp.where(first, high, low)


def finish_kernel(scale, rounds, core, mine, other, field, basis, factor, gram, inverse, a_high, a_low):
    width = gram.shape[0]
    mid, quarter = width // 2, width // 4
    first = core[0] == 0
    low = jnp.where(first, mine[...], other[...])
    high = jnp.where(first, other[...], mine[...])
    corner = jnp.concatenate([low[mid:], high[mid:]], axis=0)
    gram[:mid, :mid] = low[:mid]
    gram[mid:, mid:] = high[:mid]
    gram[mid:, :mid] = corner
    gram[:mid, mid:] = corner.T
    matrix = gram[...]
    row = lax.broadcasted_iota(jnp.int32, matrix.shape, 0)
    column = lax.broadcasted_iota(jnp.int32, matrix.shape, 1)
    eye = (row == column).astype(F32)
    diagonal = matrix * eye
    down = lax.rsqrt(jnp.sum(diagonal, axis=1, keepdims=True))
    along = lax.rsqrt(jnp.sum(diagonal, axis=0, keepdims=True))
    unit = matrix * down * along
    parts = halves(unit)
    a_high[...], a_low[...] = parts

    def correction(error):
        return jnp.where(row > column, error, 0.5 * eye * error).astype(BF16)

    now = (eye - jnp.where(row > column, unit, 0.0)).astype(BF16)
    for _ in range(rounds):
        error = dot(dot(now, a_high[...]).astype(BF16), now, NT) - eye
        now = (now.astype(F32) - dot(correction(error), now)).astype(BF16)
    exact = now.astype(F32)
    applied = dot(now, a_high[...]) + dot(now, a_low[...])
    applied_high, applied_low = halves(applied)
    error = dot(applied_high, now, NT) + dot(applied_low, now, NT) - eye
    exact = exact - dot(correction(error), now)
    full = halves(exact)
    error = dot3(halves(dot3(full, (a_high[...], a_low[...]))), full, NT) - eye
    inverse[...] = (exact - dot(correction(error), full[0])) * along
    left = jnp.sum(error * error)

    @pl.when(jnp.logical_not(left < 1e-4))
    def _():
        inverse[...] = eye
        across = lax.broadcasted_iota(jnp.int32, (1, width), 1)
        down_at = lax.broadcasted_iota(jnp.int32, (width, 1), 0)

        def eliminate(k, _):
            pivot_row = gram[pl.ds(k, 1), :]
            pivot = jnp.sum(jnp.where(across == k, pivot_row, 0.0), axis=1, keepdims=True)
            scaled = pivot_row * lax.rsqrt(pivot)
            now = gram[...]
            below = jnp.sum(jnp.where(column == k, now, 0.0), axis=1, keepdims=True)
            below = jnp.where(down_at > k, below * lax.rsqrt(pivot), 0.0)
            done = inverse[pl.ds(k, 1), :] * lax.rsqrt(pivot)
            gram[...] = now - below * scaled
            inverse[...] = inverse[...] - below * done
            inverse[pl.ds(k, 1), :] = done
            return 0

        lax.fori_loop(0, width, eliminate, 0)

    solved = halves(inverse[...])
    upper = dot3(solved, halves(matrix)) * (1.0 / scale)
    factor[...] = jnp.where(row <= column, upper, 0.0)
    basis[...] = (dot3(solved, halves(field[...])) * scale).T


def all_reduced(value):
    count, cols = lax.axis_size("tile"), lax.axis_size("col")
    if count & (count - 1):
        return lax.psum(value, "tile")
    jumps = []
    for bit in range(count.bit_length() - 1):
        jumps.append(1 << bit if bit < 2 else 3 << (bit - 1))
    for step, jump in enumerate(jumps):
        other = jumps[1 - step] if step < 2 and len(jumps) > 1 else jump
        pairs = []
        for i in range(count):
            for c in range(cols):
                pairs.append((i * cols + c, (i ^ (jump, other)[c % 2]) * cols + c))
        value = value + lax.ppermute(value, ("tile", "col"), pairs)
    return value


def on_device(jacobian, footprint, live, noise_weight, probes):
    slots, reach, rows, cells = jacobian.shape
    width = probes.shape[2]
    half = slots // lax.axis_size("col")
    cap = slots + MAX_GROUP
    col = lax.axis_index("col").astype(jnp.int32)
    core = jnp.stack([col, lax.rem(lax.axis_index("tile").astype(jnp.int32), 2)])
    mine = probes[0]

    def smem(n):
        return jax.ShapeDtypeStruct((n,), jnp.int32)

    ids, own, every = kernel_call(
        functools.partial(list_kernel, cap, half),
        (smem(len(OFFSETS) * cap), smem(len(OFFSETS)), smem(len(OFFSETS))),
        [SMEM] * 3,
        (SMEM,) * 3,
    )(footprint, live, core)

    back, ahead = spread(mine, -2), spread(mine, 2)
    near = [mine, back, ahead, swapped(mine), swapped(back)]
    near[4], ids = lax.optimization_barrier((near[4], ids))
    far = [flipped(piece) for piece in near]
    jac_far = flipped(jacobian)

    share = 2 * half * reach * rows * 2 * cells * width
    weighted = kernel_call(
        functools.partial(forward_kernel, cap),
        jax.ShapeDtypeStruct((half, width, rows), BF16),
        [SMEM] * 3 + [VMEM] * 13,
        VMEM,
        [pltpu.VMEM((len(OFFSETS), 2 * cells, width), BF16), pltpu.VMEM((half + 1, rows, width), F32)],
        flops=share,
    )(ids, own, core, jacobian, jac_far, *near, *far, noise_weight)
    weighted = kernel_call(
        gather_kernel,
        jax.ShapeDtypeStruct((2 * half + 1, width, rows), BF16),
        [VMEM] * 2,
        VMEM,
    )(weighted, flipped(weighted))

    plain = jax.ShapeDtypeStruct((width, cells), F32)
    message = jax.ShapeDtypeStruct((width + PAD, cells), jnp.int16)

    def bucket(role, coded):
        return kernel_call(
            functools.partial(backward_kernel, role, coded, cap),
            message if coded else plain,
            [SMEM] * 3 + [VMEM] * 2,
            VMEM,
            [pltpu.VMEM((width, cells), F32)],
        )(ids, every, core, jacobian, weighted)

    beyond = swapped(bucket("beyond", True))
    ahead = spread(bucket("ahead", True), -2)
    partner = swapped(bucket("partner", True))
    back = kernel_call(merge_kernel, message, [VMEM] * 2, VMEM)(bucket("back", False), beyond)
    arrived = [ahead, partner, spread(back, 2)]
    packed = jax.ShapeDtypeStruct((3 * width // 4, width // 2), F32)
    field, keep, send = kernel_call(
        field_kernel,
        (plain, packed, packed),
        [SMEM] + [VMEM] * 5,
        (VMEM,) * 3,
    )(core, mine, bucket("own", False), *arrived)
    summed = all_reduced(keep + flipped(send))
    scale = math.sqrt(cells * lax.axis_size("col") * lax.axis_size("tile"))
    square = jax.ShapeDtypeStruct((width, width), F32)
    basis, factor = kernel_call(
        functools.partial(finish_kernel, scale, 2),
        (jax.ShapeDtypeStruct((cells, width), F32), square),
        [SMEM] + [VMEM] * 3,
        (VMEM,) * 2,
        [pltpu.VMEM((width, width), F32)] * 2 + [pltpu.VMEM((width, width), BF16)] * 2,
    )(core, summed, flipped(summed), field)
    return (basis[None], factor)


def solution(mesh):
    placed = (
        P(("groups", "tile"), None, None, "col"),
        P(("groups", "tile"), None),
        P(("groups", "tile")),
        P(("groups", "tile"), None),
        P(("groups", "tile"), "col", None),
    )
    return jax.shard_map(
        on_device,
        mesh=mesh,
        in_specs=placed,
        out_specs=(P(("groups", "tile"), "col", None), P("groups", None)),
        check_vma=False,
    )
```

```python
import functools
import math

import jax
import jax.numpy as jnp
from jax import lax
from jax.experimental import pallas as pl
from jax.experimental.pallas import tpu as pltpu
from jax.sharding import PartitionSpec as P

F32 = jnp.float32
BF16 = jnp.bfloat16
NN = (((1,), (0,)), ((), ()))
NT = (((1,), (1,)), ((), ()))
OFFSETS = (-2, -1, 0, 1, 2)
PAD = 16
LIMIT = 16 << 20
VMEM = pl.BlockSpec(memory_space=pltpu.VMEM)
SMEM = pl.BlockSpec(memory_space=pltpu.SMEM)
HBM = pl.BlockSpec(memory_space=pltpu.HBM)
STEP = 4


def kernel_call(body, out_shape, in_specs, out_specs, scratch=(), flops=1024, nbytes=1024):
    return pl.pallas_call(
        body,
        out_shape=out_shape,
        in_specs=in_specs,
        out_specs=out_specs,
        scratch_shapes=list(scratch),
        compiler_params=pltpu.CompilerParams(vmem_limit_bytes=LIMIT),
        cost_estimate=pl.CostEstimate(flops=flops, bytes_accessed=nbytes, transcendentals=0),
    )


def dot(a, b, dims=NN):
    return lax.dot_general(a, b, dims, preferred_element_type=F32)


def halves(a):
    high = a.astype(BF16)
    return high, (a - high.astype(F32)).astype(BF16)


def dot3(a, b, dims=NN):
    a_high, a_low = a
    b_high, b_low = b
    return dot(a_high, b_high, dims) + (dot(a_high, b_low, dims) + dot(a_low, b_high, dims))


held = pltpu.with_memory_space_constraint


def shifted(value, axis, steps):
    count = lax.axis_size(axis)
    pairs = [(source, (source + steps) % count) for source in range(count)]
    return lax.ppermute(value, axis, pairs)


def flipped(value):
    return shifted(value, "col", 1)


def swapped(value):
    return lax.ppermute(value, "tile", [(i, i ^ 1) for i in range(lax.axis_size("tile"))])


def spread(value, steps):
    count = lax.axis_size("tile")
    return lax.ppermute(value, "tile", [(i, (i + (steps, -steps)[i % 2]) % count) for i in range(count)])


ROLES = ("own", "back", "ahead", "partner", "beyond")


def core_index():
    return lax.axis_index("col").astype(jnp.int32)


def place_of(role):
    parity = lax.rem(lax.axis_index("tile").astype(jnp.int32), 2)
    return {
        "own": 2,
        "back": 4 - 4 * parity,
        "ahead": 4 * parity,
        "partner": 3 - 2 * parity,
        "beyond": 1 + 2 * parity,
    }[role]


def list_kernel(cap, half, footprint, live, table):
    reach, slots = footprint.shape
    core = core_index()
    counts = len(OFFSETS) * cap
    for o in range(len(OFFSETS)):
        table[counts + o] = 0

    def step(j, _):
        slot = lax.rem(j + core * half, slots)
        alive = (slot < live[0]).astype(jnp.int32)
        for f in range(reach):
            o = footprint[f, slot]
            n = table[counts + o]
            table[o * cap + n] = j * 4 + f
            table[counts + o] = n + alive
        return 0

    lax.fori_loop(0, slots, step, 0)


def stage_kernel(value, out, sem):
    copy = pltpu.make_async_copy(value, out, sem)
    copy.start()
    copy.wait()


def early_kernel(footprint, jac_near, jac_far, *rest):
    count = len(ROLES) - 1
    near, far = rest[:count], rest[count : 2 * count]
    images, aside, window = rest[2 * count :]
    slots = images.shape[0]
    _, reach, _, cells = jac_near.shape
    base = core_index() * slots
    for i in range(count):
        o = place_of(ROLES[i])
        window[o, :cells] = near[i][...]
        window[o, cells:] = far[i][...]
    last = place_of(ROLES[count])
    window[last] = jnp.zeros(window.shape[1:], BF16)
    for j in range(slots):
        places = [footprint[f, base + j] for f in range(reach)]
        pieces = [jac[base + j, f] for f in range(reach) for jac in (jac_near, jac_far)]
        bands = [window[place] for place in places]
        images[j] = dot(jnp.concatenate(pieces, axis=1), jnp.concatenate(bands, axis=0))
        chosen = sum(f * (places[f] == last).astype(jnp.int32) for f in range(reach))
        found = sum((place == last).astype(jnp.int32) for place in places)
        for side, jac in enumerate((jac_near, jac_far)):
            block = jac[base + j, chosen]
            aside[j, :, side * cells : (side + 1) * cells] = jnp.where(found > 0, block, jnp.zeros_like(block))


def late_kernel(live, images, aside, near, far, noise, out):
    half, _, rows = out.shape
    base = core_index() * half
    band = jnp.concatenate([near[...], far[...]], axis=0)
    size = half // 2
    for first in range(0, half, size):
        product = dot(jnp.concatenate([aside[first + j] for j in range(size)], axis=0), band)
        for j in range(size):
            slot = base + first + j
            scale = noise[pl.ds(slot, 1), :] * (slot < live[0]).astype(F32)
            image = images[first + j] + product[j * rows : (j + 1) * rows]
            out[first + j] = (image.T * scale).astype(BF16)


def gather_kernel(mine, other, out):
    half = mine.shape[0]

    def step(j, _):
        out[j] = mine[j]
        out[half + j] = other[j]
        return 0

    lax.fori_loop(0, half, step, 0)
    out[2 * half] = jnp.zeros(out.shape[1:], BF16)


def encode(value, out):
    width = value.shape[0]
    top = jnp.max(jnp.abs(value), axis=0, keepdims=True)
    power = jnp.clip(jnp.floor(jnp.log2(jnp.maximum(top, 1e-30))) + 1.0, -96.0, 96.0)
    coded = jnp.clip(jnp.round(value * jnp.exp2(15.0 - power)), -32767.0, 32767.0)
    out[:width] = coded.astype(jnp.int32).astype(jnp.int16)
    rows = jnp.broadcast_to(power.astype(jnp.int32), (PAD, power.shape[1]))
    out[width:] = rows.astype(jnp.int16)


def decode(part):
    width = part.shape[0] - PAD
    power = part[width:].astype(jnp.int32).astype(F32)[:1]
    return part[:width].astype(jnp.int32).astype(F32) * jnp.exp2(power - 15.0)


def backward_kernel(roles, coded, cap, table, jac, weighted, *rest):
    outs, total = rest[:-1], rest[-1]
    slots = jac.shape[0]
    half = slots // 2
    counts = len(OFFSETS) * cap
    core = core_index()
    for role, code_it, out in zip(roles, coded, outs, strict=True):
        o = place_of(role)
        count = table[counts + o]

        def product(size):
            left, right = [], []
            for n in range(size):
                code = jnp.where(n < count, table[o * cap + n], slots * 4)
                j, f = lax.shift_right_logical(code, 2), jnp.bitwise_and(code, 3)
                left.append(weighted[j])
                right.append(jac[lax.rem(j + core * half, slots), f])
            total[...] = dot(jnp.concatenate(left, axis=1), jnp.concatenate(right, axis=0))

        below = -1
        for size in range(slots * 3 // 8, slots + 1, STEP):
            pl.when((count > below) & (count <= size))(functools.partial(product, size))
            below = size
        if code_it:
            encode(total[...], out)
        else:
            out[...] = total[...]


def merge_kernel(value, part, out):
    encode(value[...] + decode(part), out)


def field_kernel(probes, own, *rest):
    parts, (field, keep, send) = rest[:3], rest[3:]
    width = own.shape[0]
    total = probes[...].astype(F32).T + own[...]
    for part in parts:
        total = total + decode(part)
    field[...] = total
    both = halves(total)
    gram = dot3(both, both, NT)
    mid, quarter = width // 2, width // 4
    lower = [gram[:mid, :mid], gram[mid : mid + quarter, :mid]]
    upper = [gram[mid:, mid:], gram[mid + quarter :, :mid]]
    first = core_index() == 0
    low, high = jnp.concatenate(lower, axis=0), jnp.concatenate(upper, axis=0)
    keep[...] = jnp.where(first, low, high)
    send[...] = jnp.where(first, high, low)


def finish_kernel(scale, rounds, mine, other, field, basis, factor, gram, inverse, a_high, a_low):
    width = gram.shape[0]
    mid, quarter = width // 2, width // 4
    first = core_index() == 0
    low = jnp.where(first, mine[...], other[...])
    high = jnp.where(first, other[...], mine[...])
    corner = jnp.concatenate([low[mid:], high[mid:]], axis=0)
    gram[:mid, :mid] = low[:mid]
    gram[mid:, mid:] = high[:mid]
    gram[mid:, :mid] = corner
    gram[:mid, mid:] = corner.T
    matrix = gram[...]
    row = lax.broadcasted_iota(jnp.int32, matrix.shape, 0)
    column = lax.broadcasted_iota(jnp.int32, matrix.shape, 1)
    eye = (row == column).astype(F32)
    diagonal = matrix * eye
    down = lax.rsqrt(jnp.sum(diagonal, axis=1, keepdims=True))
    along = lax.rsqrt(jnp.sum(diagonal, axis=0, keepdims=True))
    unit = matrix * down * along
    parts = halves(unit)
    a_high[...], a_low[...] = parts

    def correction(error):
        return jnp.where(row > column, error, 0.5 * eye * error).astype(BF16)

    now = (eye - jnp.where(row > column, unit, 0.0)).astype(BF16)
    for _ in range(rounds):
        error = dot(dot(now, a_high[...]).astype(BF16), now, NT) - eye
        exact = now.astype(F32) - dot(correction(error), now)
        now = exact.astype(BF16)
    full = halves(exact)
    error = dot3(halves(dot3(full, (a_high[...], a_low[...]))), full, NT) - eye
    inverse[...] = (exact - dot(correction(error), full[0])) * along
    left = jnp.sum(error * error)

    @pl.when(jnp.logical_not(left < 1e-2))
    def _():
        inverse[...] = eye
        across = lax.broadcasted_iota(jnp.int32, (1, width), 1)
        down_at = lax.broadcasted_iota(jnp.int32, (width, 1), 0)

        def eliminate(k, _):
            pivot_row = gram[pl.ds(k, 1), :]
            pivot = jnp.sum(jnp.where(across == k, pivot_row, 0.0), axis=1, keepdims=True)
            scaled = pivot_row * lax.rsqrt(pivot)
            now = gram[...]
            below = jnp.sum(jnp.where(column == k, now, 0.0), axis=1, keepdims=True)
            below = jnp.where(down_at > k, below * lax.rsqrt(pivot), 0.0)
            done = inverse[pl.ds(k, 1), :] * lax.rsqrt(pivot)
            gram[...] = now - below * scaled
            inverse[...] = inverse[...] - below * done
            inverse[pl.ds(k, 1), :] = done
            return 0

        lax.fori_loop(0, width, eliminate, 0)

    solved = halves(inverse[...])
    upper = dot3(solved, halves(matrix)) * (1.0 / scale)
    factor[...] = jnp.where(row <= column, upper, 0.0)
    basis[...] = (dot3(solved, halves(field[...])) * scale).T


def all_reduced(value):
    count = lax.axis_size("tile")
    if count & (count - 1):
        return lax.psum(value, "tile")

    def exchanged(jump):
        return lax.ppermute(value, "tile", [(i, i ^ jump) for i in range(count)])

    bit = 1
    while bit < count:
        if bit == 1 or 2 * bit == count:
            value = value + exchanged(bit)
            bit *= 2
        else:
            first, second, third = exchanged(bit), exchanged(2 * bit), exchanged(3 * bit)
            value = (value + first) + (second + third)
            bit *= 4
    return value


def on_device(jacobian, footprint, live, noise_weight, probes):
    slots, reach, rows, cells = jacobian.shape
    width = probes.shape[2]
    half = slots // lax.axis_size("col")
    cap = slots
    footprint = footprint.T
    mine = probes[0]

    back, ahead, partner = spread(mine, -2), spread(mine, 2), swapped(mine)
    jac_far = flipped(jacobian)
    staged = kernel_call(
        stage_kernel,
        pltpu.VMEM(jacobian.shape, BF16),
        [HBM],
        VMEM,
        [pltpu.SemaphoreType.DMA(())],
    )(held(jacobian, pltpu.HBM))
    back, staged = lax.optimization_barrier((back, staged))
    near = [mine, back, ahead, partner]
    far = [flipped(mine), flipped(back)]
    ahead, partner, _ = lax.optimization_barrier((ahead, partner, far[1]))
    far += [flipped(ahead), flipped(partner)]

    early = kernel_call(
        early_kernel,
        (
            jax.ShapeDtypeStruct((half, rows, width), F32),
            jax.ShapeDtypeStruct((half, rows, 2 * cells), BF16),
        ),
        [SMEM] + [VMEM] * 10,
        (VMEM,) * 2,
        [pltpu.VMEM((len(OFFSETS), 2 * cells, width), BF16)],
    )(footprint, held(staged, pltpu.VMEM), held(jac_far, pltpu.VMEM), *near, *far)
    beyond = swapped(back)
    weighted = kernel_call(
        late_kernel,
        jax.ShapeDtypeStruct((half, width, rows), BF16),
        [SMEM] + [VMEM] * 5,
        VMEM,
    )(live, *early, beyond, flipped(beyond), noise_weight)
    table = kernel_call(
        functools.partial(list_kernel, cap, half),
        jax.ShapeDtypeStruct((len(OFFSETS) * (cap + 1),), jnp.int32),
        [SMEM] * 2,
        SMEM,
    )(footprint, live)
    weighted = kernel_call(
        gather_kernel,
        jax.ShapeDtypeStruct((2 * half + 1, width, rows), BF16),
        [VMEM] * 2,
        VMEM,
    )(weighted, flipped(weighted))

    plain = jax.ShapeDtypeStruct((width, cells), F32)
    message = jax.ShapeDtypeStruct((width + PAD, cells), jnp.int16)

    def buckets(roles, coded, weighted):
        return kernel_call(
            functools.partial(backward_kernel, roles, coded, cap),
            [message if code_it else plain for code_it in coded],
            [SMEM] + [VMEM] * 2,
            [VMEM] * len(roles),
            [pltpu.VMEM((width, cells), F32)],
        )(table, held(staged, pltpu.VMEM), weighted)

    beyond = buckets(("beyond",), (True,), weighted)[0]
    beyond, weighted = lax.optimization_barrier((beyond, weighted))
    partner = buckets(("partner",), (True,), weighted)[0]
    partner, weighted = lax.optimization_barrier((partner, weighted))
    back, ahead = buckets(("back", "ahead"), (False, True), weighted)
    back = kernel_call(merge_kernel, message, [VMEM] * 2, VMEM)(back, swapped(beyond))
    back, ahead, weighted = lax.optimization_barrier((back, ahead, weighted))
    arrived = [spread(back, 2), spread(ahead, -2), swapped(partner)]
    own = buckets(("own",), (False,), weighted)[0]
    packed = jax.ShapeDtypeStruct((3 * width // 4, width // 2), F32)
    field, keep, send = kernel_call(
        field_kernel,
        (plain, packed, packed),
        [VMEM] * 5,
        (VMEM,) * 3,
    )(mine, own, *arrived)
    summed = all_reduced(keep + flipped(send))
    scale = math.sqrt(cells * lax.axis_size("col") * lax.axis_size("tile"))
    square = jax.ShapeDtypeStruct((width, width), F32)
    basis, factor = kernel_call(
        functools.partial(finish_kernel, scale, 2),
        (jax.ShapeDtypeStruct((cells, width), F32), square),
        [VMEM] * 3,
        (VMEM,) * 2,
        [pltpu.VMEM((width, width), F32)] * 2 + [pltpu.VMEM((width, width), BF16)] * 2,
    )(summed, flipped(summed), field)
    return (basis[None], factor)


def solution(mesh):
    placed = (
        P(("groups", "tile"), None, None, "col"),
        P(("groups", "tile"), None),
        P(("groups", "tile")),
        P(("groups", "tile"), None),
        P(("groups", "tile"), "col", None),
    )
    return jax.shard_map(
        on_device,
        mesh=mesh,
        in_specs=placed,
        out_specs=(P(("groups", "tile"), "col", None), P("groups", None)),
        check_vma=False,
    )
```

```python
import functools
import math

import jax
import jax.numpy as jnp
from jax import lax
from jax.experimental import pallas as pl
from jax.experimental.pallas import tpu as pltpu
from jax.sharding import PartitionSpec as P

F32 = jnp.float32
BF16 = jnp.bfloat16
NN = (((1,), (0,)), ((), ()))
NT = (((1,), (1,)), ((), ()))
OFFSETS = (-2, -1, 0, 1, 2)
PAD = 16
LIMIT = 16 << 20
VMEM = pl.BlockSpec(memory_space=pltpu.VMEM)
SMEM = pl.BlockSpec(memory_space=pltpu.SMEM)
HBM = pl.BlockSpec(memory_space=pltpu.HBM)
STEP = 4


def kernel_call(body, out_shape, in_specs, out_specs, scratch=(), flops=1024, nbytes=1024):
    return pl.pallas_call(
        body,
        out_shape=out_shape,
        in_specs=in_specs,
        out_specs=out_specs,
        scratch_shapes=list(scratch),
        compiler_params=pltpu.CompilerParams(vmem_limit_bytes=LIMIT),
        cost_estimate=pl.CostEstimate(flops=flops, bytes_accessed=nbytes, transcendentals=0),
    )


def dot(a, b, dims=NN):
    return lax.dot_general(a, b, dims, preferred_element_type=F32)


def halves(a):
    high = a.astype(BF16)
    return high, (a - high.astype(F32)).astype(BF16)


def dot3(a, b, dims=NN):
    a_high, a_low = a
    b_high, b_low = b
    return dot(a_high, b_high, dims) + (dot(a_high, b_low, dims) + dot(a_low, b_high, dims))


held = pltpu.with_memory_space_constraint


def shifted(value, axis, steps):
    count = lax.axis_size(axis)
    pairs = [(source, (source + steps) % count) for source in range(count)]
    return lax.ppermute(value, axis, pairs)


def flipped(value):
    return shifted(value, "col", 1)


def swapped(value):
    return lax.ppermute(value, "tile", [(i, i ^ 1) for i in range(lax.axis_size("tile"))])


def spread(value, steps):
    count = lax.axis_size("tile")
    return lax.ppermute(value, "tile", [(i, (i + (steps, -steps)[i % 2]) % count) for i in range(count)])


ROLES = ("own", "back", "ahead", "partner", "beyond")


def core_index():
    return lax.axis_index("col").astype(jnp.int32)


def place_of(role):
    parity = lax.rem(lax.axis_index("tile").astype(jnp.int32), 2)
    return {
        "own": 2,
        "back": 4 - 4 * parity,
        "ahead": 4 * parity,
        "partner": 3 - 2 * parity,
        "beyond": 1 + 2 * parity,
    }[role]


def list_kernel(cap, half, footprint, live, table):
    reach, slots = footprint.shape
    core = core_index()
    counts = len(OFFSETS) * cap
    for o in range(len(OFFSETS)):
        table[counts + o] = 0

    def step(j, _):
        slot = lax.rem(j + core * half, slots)
        alive = (slot < live[0]).astype(jnp.int32)
        for f in range(reach):
            o = footprint[f, slot]
            n = table[counts + o]
            table[o * cap + n] = j * 4 + f
            table[counts + o] = n + alive
        return 0

    lax.fori_loop(0, slots, step, 0)


def stage_kernel(value, out, sem):
    copy = pltpu.make_async_copy(value, out, sem)
    copy.start()
    copy.wait()


def early_kernel(footprint, jac_near, jac_far, *rest):
    count = len(ROLES) - 1
    near, far = rest[:count], rest[count : 2 * count]
    images, aside, window = rest[2 * count :]
    slots = images.shape[0]
    _, reach, _, cells = jac_near.shape
    base = core_index() * slots
    for i in range(count):
        o = place_of(ROLES[i])
        window[o, :cells] = near[i][...]
        window[o, cells:] = far[i][...]
    last = place_of(ROLES[count])
    window[last] = jnp.zeros(window.shape[1:], BF16)
    for j in range(slots):
        places = [footprint[f, base + j] for f in range(reach)]
        pieces = [jac[base + j, f] for f in range(reach) for jac in (jac_near, jac_far)]
        bands = [window[place] for place in places]
        images[j] = dot(jnp.concatenate(pieces, axis=1), jnp.concatenate(bands, axis=0))
        chosen = sum(f * (places[f] == last).astype(jnp.int32) for f in range(reach))
        found = sum((place == last).astype(jnp.int32) for place in places)
        for side, jac in enumerate((jac_near, jac_far)):
            block = jac[base + j, chosen]
            aside[j, :, side * cells : (side + 1) * cells] = jnp.where(found > 0, block, jnp.zeros_like(block))


def gather_kernel(mine, other, out):
    half = mine.shape[0]

    def step(j, _):
        out[j] = mine[j]
        out[half + j] = other[j]
        return 0

    lax.fori_loop(0, half, step, 0)
    out[2 * half] = jnp.zeros(out.shape[1:], BF16)


def encode(value, out):
    width = value.shape[0]
    top = jnp.max(jnp.abs(value), axis=0, keepdims=True)
    power = jnp.clip(jnp.floor(jnp.log2(jnp.maximum(top, 1e-30))) + 1.0, -96.0, 96.0)
    coded = jnp.clip(jnp.round(value * jnp.exp2(15.0 - power)), -32767.0, 32767.0)
    out[:width] = coded.astype(jnp.int32).astype(jnp.int16)
    rows = jnp.broadcast_to(power.astype(jnp.int32), (PAD, power.shape[1]))
    out[width:] = rows.astype(jnp.int16)


def decode(part):
    width = part.shape[0] - PAD
    power = part[width:].astype(jnp.int32).astype(F32)[:1]
    return part[:width].astype(jnp.int32).astype(F32) * jnp.exp2(power - 15.0)


def late_kernel(live, footprint, images, aside, jac_near, jac_far, near, far, noise, out, kept, sent):
    half, width, rows = out.shape
    reach, cells = jac_near.shape[1], jac_near.shape[3]
    base = core_index() * half
    band = jnp.concatenate([near[...], far[...]], axis=0)
    size = half // 2
    for first in range(0, half, size):
        product = dot(jnp.concatenate([aside[first + j] for j in range(size)], axis=0), band)
        for j in range(size):
            slot = base + first + j
            scale = noise[pl.ds(slot, 1), :] * (slot < live[0]).astype(F32)
            image = images[first + j] + product[j * rows : (j + 1) * rows]
            out[first + j] = (image.T * scale).astype(BF16)

    left = jnp.concatenate([out[j] for j in range(half)], axis=1)
    total = dot(left, jnp.concatenate([aside[j] for j in range(half)], axis=0))
    kept[0] = total[:, :cells]
    encode(total[:, cells:], sent.at[0])
    ahead = place_of("ahead")
    left, right = [], []
    for j in range(half):
        places = [footprint[f, base + j] for f in range(reach)]
        chosen = sum(f * (places[f] == ahead).astype(jnp.int32) for f in range(reach))
        found = sum((place == ahead).astype(jnp.int32) for place in places)
        block = out[j]
        left.append(jnp.where(found > 0, block, jnp.zeros_like(block)))
        right.append(jnp.concatenate([jac_near[base + j, chosen], jac_far[base + j, chosen]], axis=1))
    total = dot(jnp.concatenate(left, axis=1), jnp.concatenate(right, axis=0))
    kept[1] = total[:, :cells]
    encode(total[:, cells:], sent.at[1])


def backward_kernel(roles, coded, cap, table, jac, weighted, *rest):
    outs, total = rest[:-1], rest[-1]
    slots = jac.shape[0]
    half = slots // 2
    counts = len(OFFSETS) * cap
    core = core_index()
    for role, code_it, out in zip(roles, coded, outs, strict=True):
        o = place_of(role)
        count = table[counts + o]

        def product(size):
            left, right = [], []
            for n in range(size):
                code = jnp.where(n < count, table[o * cap + n], slots * 4)
                j, f = lax.shift_right_logical(code, 2), jnp.bitwise_and(code, 3)
                left.append(weighted[j])
                right.append(jac[lax.rem(j + core * half, slots), f])
            total[...] = dot(jnp.concatenate(left, axis=1), jnp.concatenate(right, axis=0))

        below = -1
        for size in range(slots * 3 // 8, slots + 1, STEP):
            pl.when((count > below) & (count <= size))(functools.partial(product, size))
            below = size
        if code_it:
            encode(total[...], out)
        else:
            out[...] = total[...]


def merge_kernel(value, part, out):
    encode(value[...] + decode(part), out)


def merge_two_kernel(kept, sent, first, second):
    encode(kept[0] + decode(sent.at[0]), first)
    encode(kept[1] + decode(sent.at[1]), second)


def field_kernel(probes, own, *rest):
    parts, (field, keep, send) = rest[:3], rest[3:]
    width = own.shape[0]
    total = probes[...].astype(F32).T + own[...]
    for part in parts:
        total = total + decode(part)
    field[...] = total
    both = halves(total)
    gram = dot3(both, both, NT)
    mid, quarter = width // 2, width // 4
    lower = [gram[:mid, :mid], gram[mid : mid + quarter, :mid]]
    upper = [gram[mid:, mid:], gram[mid + quarter :, :mid]]
    first = core_index() == 0
    low, high = jnp.concatenate(lower, axis=0), jnp.concatenate(upper, axis=0)
    keep[...] = jnp.where(first, low, high)
    send[...] = jnp.where(first, high, low)


def finish_kernel(scale, rounds, mine, other, field, basis, factor, gram, inverse, a_high, a_low):
    width = gram.shape[0]
    mid, quarter = width // 2, width // 4
    first = core_index() == 0
    low = jnp.where(first, mine[...], other[...])
    high = jnp.where(first, other[...], mine[...])
    corner = jnp.concatenate([low[mid:], high[mid:]], axis=0)
    gram[:mid, :mid] = low[:mid]
    gram[mid:, mid:] = high[:mid]
    gram[mid:, :mid] = corner
    gram[:mid, mid:] = corner.T
    matrix = gram[...]
    row = lax.broadcasted_iota(jnp.int32, matrix.shape, 0)
    column = lax.broadcasted_iota(jnp.int32, matrix.shape, 1)
    eye = (row == column).astype(F32)
    diagonal = matrix * eye
    down = lax.rsqrt(jnp.sum(diagonal, axis=1, keepdims=True))
    along = lax.rsqrt(jnp.sum(diagonal, axis=0, keepdims=True))
    unit = matrix * down * along
    parts = halves(unit)
    a_high[...], a_low[...] = parts

    def correction(error):
        return jnp.where(row > column, error, 0.5 * eye * error).astype(BF16)

    now = (eye - jnp.where(row > column, unit, 0.0)).astype(BF16)
    for _ in range(rounds):
        error = dot(dot(now, a_high[...]).astype(BF16), now, NT) - eye
        exact = now.astype(F32) - dot(correction(error), now)
        now = exact.astype(BF16)
    full = halves(exact)
    error = dot3(halves(dot3(full, (a_high[...], a_low[...]))), full, NT) - eye
    inverse[...] = (exact - dot(correction(error), full[0])) * along
    left = jnp.sum(error * error)

    @pl.when(jnp.logical_not(left < 1e-2))
    def _():
        inverse[...] = eye
        across = lax.broadcasted_iota(jnp.int32, (1, width), 1)
        down_at = lax.broadcasted_iota(jnp.int32, (width, 1), 0)

        def eliminate(k, _):
            pivot_row = gram[pl.ds(k, 1), :]
            pivot = jnp.sum(jnp.where(across == k, pivot_row, 0.0), axis=1, keepdims=True)
            scaled = pivot_row * lax.rsqrt(pivot)
            now = gram[...]
            below = jnp.sum(jnp.where(column == k, now, 0.0), axis=1, keepdims=True)
            below = jnp.where(down_at > k, below * lax.rsqrt(pivot), 0.0)
            done = inverse[pl.ds(k, 1), :] * lax.rsqrt(pivot)
            gram[...] = now - below * scaled
            inverse[...] = inverse[...] - below * done
            inverse[pl.ds(k, 1), :] = done
            return 0

        lax.fori_loop(0, width, eliminate, 0)

    solved = halves(inverse[...])
    upper = dot3(solved, halves(matrix)) * (1.0 / scale)
    factor[...] = jnp.where(row <= column, upper, 0.0)
    basis[...] = (dot3(solved, halves(field[...])) * scale).T


def all_reduced(value):
    count = lax.axis_size("tile")
    if count & (count - 1):
        return lax.psum(value, "tile")

    def exchanged(jump):
        return lax.ppermute(value, "tile", [(i, i ^ jump) for i in range(count)])

    bit = 1
    while bit < count:
        if bit == 1 or 2 * bit == count:
            value = value + exchanged(bit)
            bit *= 2
        else:
            first, second, third = exchanged(bit), exchanged(2 * bit), exchanged(3 * bit)
            value = (value + first) + (second + third)
            bit *= 4
    return value


def on_device(jacobian, footprint, live, noise_weight, probes):
    slots, reach, rows, cells = jacobian.shape
    width = probes.shape[2]
    half = slots // lax.axis_size("col")
    cap = slots
    footprint = footprint.T
    mine = probes[0]

    back, ahead, partner = spread(mine, -2), spread(mine, 2), swapped(mine)
    jac_far = flipped(jacobian)
    staged = kernel_call(
        stage_kernel,
        pltpu.VMEM(jacobian.shape, BF16),
        [HBM],
        VMEM,
        [pltpu.SemaphoreType.DMA(())],
    )(held(jacobian, pltpu.HBM))
    back, staged = lax.optimization_barrier((back, staged))
    near = [mine, back, ahead, partner]
    far = [flipped(mine), flipped(back)]
    ahead, partner, _ = lax.optimization_barrier((ahead, partner, far[1]))
    far += [flipped(ahead), flipped(partner)]

    early = kernel_call(
        early_kernel,
        (
            jax.ShapeDtypeStruct((half, rows, width), F32),
            jax.ShapeDtypeStruct((half, rows, 2 * cells), BF16),
        ),
        [SMEM] + [VMEM] * 10,
        (VMEM,) * 2,
        [pltpu.VMEM((len(OFFSETS), 2 * cells, width), BF16)],
    )(footprint, held(staged, pltpu.VMEM), held(jac_far, pltpu.VMEM), *near, *far)
    table = kernel_call(
        functools.partial(list_kernel, cap, half),
        jax.ShapeDtypeStruct((len(OFFSETS) * (cap + 1),), jnp.int32),
        [SMEM] * 2,
        SMEM,
    )(footprint, live)
    beyond, table = lax.optimization_barrier((swapped(back), table))
    plain = jax.ShapeDtypeStruct((width, cells), F32)
    message = jax.ShapeDtypeStruct((width + PAD, cells), jnp.int16)
    weighted, kept, sent = kernel_call(
        late_kernel,
        (
            jax.ShapeDtypeStruct((half, width, rows), BF16),
            jax.ShapeDtypeStruct((2,) + plain.shape, F32),
            jax.ShapeDtypeStruct((2,) + message.shape, jnp.int16),
        ),
        [SMEM] * 2 + [VMEM] * 7,
        (VMEM,) * 3,
    )(live, footprint, *early, held(staged, pltpu.VMEM), held(jac_far, pltpu.VMEM), beyond, flipped(beyond), noise_weight)
    beyond, ahead = kernel_call(merge_two_kernel, (message, message), [VMEM] * 2, (VMEM,) * 2)(kept, flipped(sent))
    beyond, ahead, weighted = lax.optimization_barrier((beyond, ahead, weighted))
    beyond, ahead = swapped(beyond), spread(ahead, -2)
    weighted = kernel_call(
        gather_kernel,
        jax.ShapeDtypeStruct((2 * half + 1, width, rows), BF16),
        [VMEM] * 2,
        VMEM,
    )(weighted, flipped(weighted))

    def buckets(roles, coded, weighted):
        return kernel_call(
            functools.partial(backward_kernel, roles, coded, cap),
            [message if code_it else plain for code_it in coded],
            [SMEM] + [VMEM] * 2,
            [VMEM] * len(roles),
            [pltpu.VMEM((width, cells), F32)],
        )(table, held(staged, pltpu.VMEM), weighted)

    back, partner = buckets(("back", "partner"), (False, True), weighted)
    back = kernel_call(merge_kernel, message, [VMEM] * 2, VMEM)(back, beyond)
    back, partner, weighted = lax.optimization_barrier((back, partner, weighted))
    arrived = [spread(back, 2), ahead, swapped(partner)]
    own = buckets(("own",), (False,), weighted)[0]
    packed = jax.ShapeDtypeStruct((3 * width // 4, width // 2), F32)
    field, keep, send = kernel_call(
        field_kernel,
        (plain, packed, packed),
        [VMEM] * 5,
        (VMEM,) * 3,
    )(mine, own, *arrived)
    summed = all_reduced(keep + flipped(send))
    scale = math.sqrt(cells * lax.axis_size("col") * lax.axis_size("tile"))
    square = jax.ShapeDtypeStruct((width, width), F32)
    basis, factor = kernel_call(
        functools.partial(finish_kernel, scale, 2),
        (jax.ShapeDtypeStruct((cells, width), F32), square),
        [VMEM] * 3,
        (VMEM,) * 2,
        [pltpu.VMEM((width, width), F32)] * 2 + [pltpu.VMEM((width, width), BF16)] * 2,
    )(summed, flipped(summed), field)
    return (basis[None], factor)


def solution(mesh):
    placed = (
        P(("groups", "tile"), None, None, "col"),
        P(("groups", "tile"), None),
        P(("groups", "tile")),
        P(("groups", "tile"), None),
        P(("groups", "tile"), "col", None),
    )
    return jax.shard_map(
        on_device,
        mesh=mesh,
        in_specs=placed,
        out_specs=(P(("groups", "tile"), "col", None), P("groups", None)),
        check_vma=False,
    )
```

```python
import functools
import math

import jax
import jax.numpy as jnp
from jax import lax
from jax.experimental import pallas as pl
from jax.experimental.pallas import tpu as pltpu
from jax.sharding import PartitionSpec as P

F32 = jnp.float32
BF16 = jnp.bfloat16
NN = (((1,), (0,)), ((), ()))
NT = (((1,), (1,)), ((), ()))
OFFSETS = (-2, -1, 0, 1, 2)
PAD = 16
ROWS = 8
LIMIT = 16 << 20
VMEM = pl.BlockSpec(memory_space=pltpu.VMEM)
SMEM = pl.BlockSpec(memory_space=pltpu.SMEM)
HBM = pl.BlockSpec(memory_space=pltpu.HBM)
STEP = 4


def kernel_call(body, out_shape, in_specs, out_specs, scratch=(), flops=1024, nbytes=1024):
    return pl.pallas_call(
        body,
        out_shape=out_shape,
        in_specs=in_specs,
        out_specs=out_specs,
        scratch_shapes=list(scratch),
        compiler_params=pltpu.CompilerParams(vmem_limit_bytes=LIMIT),
        cost_estimate=pl.CostEstimate(flops=flops, bytes_accessed=nbytes, transcendentals=0),
    )


def dot(a, b, dims=NN):
    return lax.dot_general(a, b, dims, preferred_element_type=F32)


def halves(a):
    high = a.astype(BF16)
    return high, (a - high.astype(F32)).astype(BF16)


def dot3(a, b, dims=NN):
    a_high, a_low = a
    b_high, b_low = b
    return dot(a_high, b_high, dims) + (dot(a_high, b_low, dims) + dot(a_low, b_high, dims))


held = pltpu.with_memory_space_constraint


def shifted(value, axis, steps):
    count = lax.axis_size(axis)
    pairs = [(source, (source + steps) % count) for source in range(count)]
    return lax.ppermute(value, axis, pairs)


def flipped(value):
    return shifted(value, "col", 1)


def swapped(value):
    return lax.ppermute(value, "tile", [(i, i ^ 1) for i in range(lax.axis_size("tile"))])


def spread(value, steps):
    count = lax.axis_size("tile")
    return lax.ppermute(value, "tile", [(i, (i + (steps, -steps)[i % 2]) % count) for i in range(count)])


ROLES = ("own", "back", "ahead", "partner", "beyond")


def core_index():
    return lax.axis_index("col").astype(jnp.int32)


def place_of(role):
    parity = lax.rem(lax.axis_index("tile").astype(jnp.int32), 2)
    return {
        "own": 2,
        "back": 4 - 4 * parity,
        "ahead": 4 * parity,
        "partner": 3 - 2 * parity,
        "beyond": 1 + 2 * parity,
    }[role]


def list_kernel(cap, half, footprint, live, table):
    reach, slots = footprint.shape
    core = core_index()
    counts = len(OFFSETS) * cap
    for o in range(len(OFFSETS)):
        table[counts + o] = 0

    def step(j, _):
        slot = lax.rem(j + core * half, slots)
        alive = (slot < live[0]).astype(jnp.int32)
        for f in range(reach):
            o = footprint[f, slot]
            n = table[counts + o]
            table[o * cap + n] = j * 4 + f
            table[counts + o] = n + alive
        return 0

    lax.fori_loop(0, slots, step, 0)


def stage_kernel(value, out, sem):
    copy = pltpu.make_async_copy(value, out, sem)
    copy.start()
    copy.wait()


def early_kernel(footprint, jac_near, jac_far, *rest):
    count = len(ROLES) - 1
    near, far = rest[:count], rest[count : 2 * count]
    images, aside, window = rest[2 * count :]
    slots = images.shape[0]
    _, reach, _, cells = jac_near.shape
    base = core_index() * slots
    for i in range(count):
        o = place_of(ROLES[i])
        window[o, :cells] = near[i][...]
        window[o, cells:] = far[i][...]
    last = place_of(ROLES[count])
    window[last] = jnp.zeros(window.shape[1:], BF16)
    for j in range(slots):
        places = [footprint[f, base + j] for f in range(reach)]
        pieces = [jac[base + j, f] for f in range(reach) for jac in (jac_near, jac_far)]
        bands = [window[place] for place in places]
        images[j] = dot(jnp.concatenate(pieces, axis=1), jnp.concatenate(bands, axis=0))
        chosen = sum(f * (places[f] == last).astype(jnp.int32) for f in range(reach))
        found = sum((place == last).astype(jnp.int32) for place in places)
        for side, jac in enumerate((jac_near, jac_far)):
            block = jac[base + j, chosen]
            aside[j, :, side * cells : (side + 1) * cells] = jnp.where(found > 0, block, jnp.zeros_like(block))


def gather_kernel(mine, other, out):
    half = mine.shape[0]

    def step(j, _):
        out[j] = mine[j]
        out[half + j] = other[j]
        return 0

    lax.fori_loop(0, half, step, 0)
    out[2 * half] = jnp.zeros(out.shape[1:], BF16)


def encode(value, out):
    width = value.shape[0]
    top = jnp.max(jnp.abs(value), axis=0, keepdims=True)
    power = jnp.clip(jnp.floor(jnp.log2(jnp.maximum(top, 1e-30))) + 1.0, -96.0, 96.0)
    coded = jnp.clip(jnp.round(value * jnp.exp2(15.0 - power)), -32767.0, 32767.0)
    out[:width] = coded.astype(jnp.int32).astype(jnp.int16)
    rows = jnp.broadcast_to(power.astype(jnp.int32), (PAD, power.shape[1]))
    out[width:] = rows.astype(jnp.int16)


def decode(part):
    width = part.shape[0] - PAD
    power = part[width:].astype(jnp.int32).astype(F32)[:1]
    return part[:width].astype(jnp.int32).astype(F32) * jnp.exp2(power - 15.0)


def late_kernel(live, footprint, images, aside, jac_near, jac_far, near, far, noise, out, kept, sent):
    half, width, rows = out.shape
    reach, cells = jac_near.shape[1], jac_near.shape[3]
    base = core_index() * half
    band = jnp.concatenate([near[...], far[...]], axis=0)
    size = half // 2
    for first in range(0, half, size):
        product = dot(jnp.concatenate([aside[first + j] for j in range(size)], axis=0), band)
        for j in range(size):
            slot = base + first + j
            scale = noise[pl.ds(slot, 1), :] * (slot < live[0]).astype(F32)
            image = images[first + j] + product[j * rows : (j + 1) * rows]
            out[first + j] = (image.T * scale).astype(BF16)

    left = jnp.concatenate([out[j] for j in range(half)], axis=1)
    total = dot(left, jnp.concatenate([aside[j] for j in range(half)], axis=0))
    kept[0] = total[:, :cells]
    encode(total[:, cells:], sent.at[0])
    ahead = place_of("ahead")
    left, right = [], []
    for j in range(half):
        places = [footprint[f, base + j] for f in range(reach)]
        chosen = sum(f * (places[f] == ahead).astype(jnp.int32) for f in range(reach))
        found = sum((place == ahead).astype(jnp.int32) for place in places)
        block = out[j]
        left.append(jnp.where(found > 0, block, jnp.zeros_like(block)))
        right.append(jnp.concatenate([jac_near[base + j, chosen], jac_far[base + j, chosen]], axis=1))
    total = dot(jnp.concatenate(left, axis=1), jnp.concatenate(right, axis=0))
    kept[1] = total[:, :cells]
    encode(total[:, cells:], sent.at[1])


def backward_kernel(roles, coded, cap, table, jac, weighted, *rest):
    outs, total = rest[:-1], rest[-1]
    slots = jac.shape[0]
    half = slots // 2
    counts = len(OFFSETS) * cap
    core = core_index()
    for role, code_it, out in zip(roles, coded, outs, strict=True):
        o = place_of(role)
        count = table[counts + o]

        def product(size):
            left, right = [], []
            for n in range(size):
                code = jnp.where(n < count, table[o * cap + n], slots * 4)
                j, f = lax.shift_right_logical(code, 2), jnp.bitwise_and(code, 3)
                left.append(weighted[j])
                right.append(jac[lax.rem(j + core * half, slots), f])
            total[...] = dot(jnp.concatenate(left, axis=1), jnp.concatenate(right, axis=0))

        below = -1
        for size in range(slots * 3 // 8, slots + 1, STEP):
            pl.when((count > below) & (count <= size))(functools.partial(product, size))
            below = size
        if code_it:
            encode(total[...], out)
        else:
            out[...] = total[...]


def merge_kernel(value, part, out):
    encode(value[...] + decode(part), out)


def merge_two_kernel(kept, sent, first, second):
    encode(kept[0] + decode(sent.at[0]), first)
    encode(kept[1] + decode(sent.at[1]), second)


def field_kernel(probes, own, *rest):
    parts, (field, keep, send) = rest[:3], rest[3:]
    width = own.shape[0]
    total = probes[...].astype(F32).T + own[...]
    for part in parts:
        total = total + decode(part)
    field[...] = total
    both = halves(total)
    gram = dot3(both, both, NT)
    mid, quarter = width // 2, width // 4
    first = core_index() == 0
    corner = gram[mid:, :mid]
    folded, ends = fold(gram[:mid, :mid], gram[mid:, mid:])
    low = jnp.concatenate([corner[:quarter], folded[:quarter], ends], axis=0)
    high = jnp.concatenate([corner[quarter:], folded[quarter:], ends], axis=0)
    keep[...] = jnp.where(first, low, high)
    send[...] = jnp.where(first, high, low)


def positions(square):
    row = lax.broadcasted_iota(jnp.int32, square.shape, 0)
    return row, lax.broadcasted_iota(jnp.int32, square.shape, 1)


def fold(lower, upper):
    row, column = positions(lower)
    diagonal = jnp.sum(jnp.where(row == column, upper, 0.0), axis=0, keepdims=True)
    return jnp.where(row >= column, lower, upper), jnp.broadcast_to(diagonal, (ROWS, lower.shape[1]))


def unfold(folded, ends):
    row, column = positions(folded)
    other = folded.T
    lower = jnp.where(row >= column, folded, other)
    upper = jnp.where(row < column, folded, other)
    return lower, jnp.where(row == column, ends[:1], upper)


def finish_kernel(scale, rounds, mine, other, field, basis, factor, gram, inverse, a_high, a_low):
    width = gram.shape[0]
    mid, quarter = width // 2, width // 4
    first = core_index() == 0
    low = jnp.where(first, mine[...], other[...])
    high = jnp.where(first, other[...], mine[...])
    folded = jnp.concatenate([low[quarter:mid], high[quarter:mid]], axis=0)
    gram[:mid, :mid], gram[mid:, mid:] = unfold(folded, low[mid:])
    corner = jnp.concatenate([low[:quarter], high[:quarter]], axis=0)
    gram[mid:, :mid] = corner
    gram[:mid, mid:] = corner.T
    matrix = gram[...]
    row = lax.broadcasted_iota(jnp.int32, matrix.shape, 0)
    column = lax.broadcasted_iota(jnp.int32, matrix.shape, 1)
    eye = (row == column).astype(F32)
    diagonal = matrix * eye
    down = lax.rsqrt(jnp.sum(diagonal, axis=1, keepdims=True))
    along = lax.rsqrt(jnp.sum(diagonal, axis=0, keepdims=True))
    unit = matrix * down * along
    parts = halves(unit)
    a_high[...], a_low[...] = parts

    def correction(error):
        return jnp.where(row > column, error, 0.5 * eye * error).astype(BF16)

    now = (eye - jnp.where(row > column, unit, 0.0)).astype(BF16)
    for _ in range(rounds):
        error = dot(dot(now, a_high[...]).astype(BF16), now, NT) - eye
        exact = now.astype(F32) - dot(correction(error), now)
        now = exact.astype(BF16)
    full = halves(exact)
    error = dot3(halves(dot3(full, (a_high[...], a_low[...]))), full, NT) - eye
    left = jnp.sum(error * error)
    solution_of = (exact - dot(correction(error), full[0])) * along
    inverse[...] = solution_of
    upper = dot3(halves(solution_of), halves(matrix)) * (1.0 / scale)
    factor[...] = jnp.where(row <= column, upper, 0.0)

    @pl.when(jnp.logical_not(left < 1e-2))
    def _():
        inverse[...] = eye
        across = lax.broadcasted_iota(jnp.int32, (1, width), 1)
        down_at = lax.broadcasted_iota(jnp.int32, (width, 1), 0)

        def eliminate(k, _):
            pivot_row = gram[pl.ds(k, 1), :]
            pivot = jnp.sum(jnp.where(across == k, pivot_row, 0.0), axis=1, keepdims=True)
            scaled = pivot_row * lax.rsqrt(pivot)
            now = gram[...]
            below = jnp.sum(jnp.where(column == k, now, 0.0), axis=1, keepdims=True)
            below = jnp.where(down_at > k, below * lax.rsqrt(pivot), 0.0)
            done = inverse[pl.ds(k, 1), :] * lax.rsqrt(pivot)
            factor[pl.ds(k, 1), :] = jnp.where(across >= k, scaled * (1.0 / scale), 0.0)
            gram[...] = now - below * scaled
            inverse[...] = inverse[...] - below * done
            inverse[pl.ds(k, 1), :] = done
            return 0

        lax.fori_loop(0, width, eliminate, 0)

    solved = halves(inverse[...])
    basis[...] = (dot3(solved, halves(field[...])) * scale).T


def all_reduced(value):
    count = lax.axis_size("tile")
    if count & (count - 1):
        return lax.psum(value, "tile")

    def exchanged(jump):
        return lax.ppermute(value, "tile", [(i, i ^ jump) for i in range(count)])

    bit = 1
    while bit < count:
        if bit == 1 or 2 * bit == count:
            value = value + exchanged(bit)
            bit *= 2
        else:
            first, second, third = exchanged(bit), exchanged(2 * bit), exchanged(3 * bit)
            value = (value + first) + (second + third)
            bit *= 4
    return value


def on_device(jacobian, footprint, live, noise_weight, probes):
    slots, reach, rows, cells = jacobian.shape
    width = probes.shape[2]
    half = slots // lax.axis_size("col")
    cap = slots
    footprint = footprint.T
    mine = probes[0]

    back, ahead, partner = spread(mine, -2), spread(mine, 2), swapped(mine)
    jac_far = flipped(jacobian)
    staged = kernel_call(
        stage_kernel,
        pltpu.VMEM(jacobian.shape, BF16),
        [HBM],
        VMEM,
        [pltpu.SemaphoreType.DMA(())],
    )(held(jacobian, pltpu.HBM))
    back, staged = lax.optimization_barrier((back, staged))
    near = [mine, back, ahead, partner]
    far = [flipped(mine), flipped(back)]
    ahead, partner, _ = lax.optimization_barrier((ahead, partner, far[1]))
    far += [flipped(ahead), flipped(partner)]

    early = kernel_call(
        early_kernel,
        (
            jax.ShapeDtypeStruct((half, rows, width), F32),
            jax.ShapeDtypeStruct((half, rows, 2 * cells), BF16),
        ),
        [SMEM] + [VMEM] * 10,
        (VMEM,) * 2,
        [pltpu.VMEM((len(OFFSETS), 2 * cells, width), BF16)],
    )(footprint, held(staged, pltpu.VMEM), held(jac_far, pltpu.VMEM), *near, *far)
    table = kernel_call(
        functools.partial(list_kernel, cap, half),
        jax.ShapeDtypeStruct((len(OFFSETS) * (cap + 1),), jnp.int32),
        [SMEM] * 2,
        SMEM,
    )(footprint, live)
    beyond, table = lax.optimization_barrier((swapped(back), table))
    plain = jax.ShapeDtypeStruct((width, cells), F32)
    message = jax.ShapeDtypeStruct((width + PAD, cells), jnp.int16)
    weighted, kept, sent = kernel_call(
        late_kernel,
        (
            jax.ShapeDtypeStruct((half, width, rows), BF16),
            jax.ShapeDtypeStruct((2,) + plain.shape, F32),
            jax.ShapeDtypeStruct((2,) + message.shape, jnp.int16),
        ),
        [SMEM] * 2 + [VMEM] * 7,
        (VMEM,) * 3,
    )(live, footprint, *early, held(staged, pltpu.VMEM), held(jac_far, pltpu.VMEM), beyond, flipped(beyond), noise_weight)
    beyond, ahead = kernel_call(merge_two_kernel, (message, message), [VMEM] * 2, (VMEM,) * 2)(kept, flipped(sent))
    beyond, ahead, weighted = lax.optimization_barrier((beyond, ahead, weighted))
    beyond, ahead = swapped(beyond), spread(ahead, -2)
    weighted = kernel_call(
        gather_kernel,
        jax.ShapeDtypeStruct((2 * half + 1, width, rows), BF16),
        [VMEM] * 2,
        VMEM,
    )(weighted, flipped(weighted))

    def buckets(roles, coded, weighted):
        return kernel_call(
            functools.partial(backward_kernel, roles, coded, cap),
            [message if code_it else plain for code_it in coded],
            [SMEM] + [VMEM] * 2,
            [VMEM] * len(roles),
            [pltpu.VMEM((width, cells), F32)],
        )(table, held(staged, pltpu.VMEM), weighted)

    back, partner = buckets(("back", "partner"), (False, True), weighted)
    back = kernel_call(merge_kernel, message, [VMEM] * 2, VMEM)(back, beyond)
    back, partner, weighted = lax.optimization_barrier((back, partner, weighted))
    arrived = [spread(back, 2), ahead, swapped(partner)]
    own = buckets(("own",), (False,), weighted)[0]
    packed = jax.ShapeDtypeStruct((width // 2 + ROWS, width // 2), F32)
    field, keep, send = kernel_call(
        field_kernel,
        (plain, packed, packed),
        [VMEM] * 5,
        (VMEM,) * 3,
    )(mine, own, *arrived)
    summed = all_reduced(keep + flipped(send))
    scale = math.sqrt(cells * lax.axis_size("col") * lax.axis_size("tile"))
    square = jax.ShapeDtypeStruct((width, width), F32)
    basis, factor = kernel_call(
        functools.partial(finish_kernel, scale, 2),
        (jax.ShapeDtypeStruct((cells, width), F32), square),
        [VMEM] * 3,
        (VMEM,) * 2,
        [pltpu.VMEM((width, width), F32)] * 2 + [pltpu.VMEM((width, width), BF16)] * 2,
    )(summed, flipped(summed), field)
    return (basis[None], factor)


def solution(mesh):
    placed = (
        P(("groups", "tile"), None, None, "col"),
        P(("groups", "tile"), None),
        P(("groups", "tile")),
        P(("groups", "tile"), None),
        P(("groups", "tile"), "col", None),
    )
    return jax.shard_map(
        on_device,
        mesh=mesh,
        in_specs=placed,
        out_specs=(P(("groups", "tile"), "col", None), P("groups", None)),
        check_vma=False,
    )
```

```python
import functools
import math

import jax
import jax.numpy as jnp
from jax import lax
from jax.experimental import pallas as pl
from jax.experimental.pallas import tpu as pltpu
from jax.sharding import PartitionSpec as P

F32 = jnp.float32
BF16 = jnp.bfloat16
NN = (((1,), (0,)), ((), ()))
NT = (((1,), (1,)), ((), ()))
OFFSETS = (-2, -1, 0, 1, 2)
PAD = 16
ROWS = 8
LIMIT = 16 << 20
VMEM = pl.BlockSpec(memory_space=pltpu.VMEM)
SMEM = pl.BlockSpec(memory_space=pltpu.SMEM)
HBM = pl.BlockSpec(memory_space=pltpu.HBM)
STEP = 4


def kernel_call(body, out_shape, in_specs, out_specs, scratch=(), flops=1024, nbytes=1024):
    return pl.pallas_call(
        body,
        out_shape=out_shape,
        in_specs=in_specs,
        out_specs=out_specs,
        scratch_shapes=list(scratch),
        compiler_params=pltpu.CompilerParams(vmem_limit_bytes=LIMIT),
        cost_estimate=pl.CostEstimate(flops=flops, bytes_accessed=nbytes, transcendentals=0),
    )


def dot(a, b, dims=NN):
    return lax.dot_general(a, b, dims, preferred_element_type=F32)


def halves(a):
    high = a.astype(BF16)
    return high, (a - high.astype(F32)).astype(BF16)


def dot3(a, b, dims=NN):
    a_high, a_low = a
    b_high, b_low = b
    return dot(a_high, b_high, dims) + (dot(a_high, b_low, dims) + dot(a_low, b_high, dims))


held = pltpu.with_memory_space_constraint


def shifted(value, axis, steps):
    count = lax.axis_size(axis)
    pairs = [(source, (source + steps) % count) for source in range(count)]
    return lax.ppermute(value, axis, pairs)


def flipped(value):
    return shifted(value, "col", 1)


def swapped(value):
    return lax.ppermute(value, "tile", [(i, i ^ 1) for i in range(lax.axis_size("tile"))])


def spread(value, steps):
    count = lax.axis_size("tile")
    return lax.ppermute(value, "tile", [(i, (i + (steps, -steps)[i % 2]) % count) for i in range(count)])


ROLES = ("own", "back", "ahead", "partner", "beyond")


def core_index():
    return lax.axis_index("col").astype(jnp.int32)


def place_of(role):
    parity = lax.rem(lax.axis_index("tile").astype(jnp.int32), 2)
    return {
        "own": 2,
        "back": 4 - 4 * parity,
        "ahead": 4 * parity,
        "partner": 3 - 2 * parity,
        "beyond": 1 + 2 * parity,
    }[role]


def list_kernel(cap, half, footprint, live, table):
    reach, slots = footprint.shape
    core = core_index()
    counts = len(OFFSETS) * cap
    places = counts + len(OFFSETS)
    table[places + reach * slots] = live[0]
    for o in range(len(OFFSETS)):
        table[counts + o] = 0

    def step(j, _):
        slot = lax.rem(j + core * half, slots)
        alive = (slot < live[0]).astype(jnp.int32)
        for f in range(reach):
            o = footprint[f, slot]
            table[places + f * slots + slot] = o
            n = table[counts + o]
            table[o * cap + n] = j * 4 + f
            table[counts + o] = n + alive
        return 0

    lax.fori_loop(0, slots, step, 0)


def stage_kernel(value, out, sem):
    copy = pltpu.make_async_copy(value, out, sem)
    copy.start()
    copy.wait()


def early_kernel(cap, table, jac_near, jac_far, *rest):
    count = len(ROLES) - 1
    near, far = rest[:count], rest[count : 2 * count]
    images, aside, window = rest[2 * count :]
    slots = images.shape[0]
    total, reach, _, cells = jac_near.shape
    base = core_index() * slots
    at = len(OFFSETS) * (cap + 1) + base
    for i in range(count):
        o = place_of(ROLES[i])
        window[o, :cells] = near[i][...]
        window[o, cells:] = far[i][...]
    last = place_of(ROLES[count])
    window[last] = jnp.zeros(window.shape[1:], BF16)
    for j in range(slots):
        places = [table[at + f * total + j] for f in range(reach)]
        pieces = [jac[base + j, f] for f in range(reach) for jac in (jac_near, jac_far)]
        bands = [window[place] for place in places]
        images[j] = dot(jnp.concatenate(pieces, axis=1), jnp.concatenate(bands, axis=0))
        chosen = sum(f * (places[f] == last).astype(jnp.int32) for f in range(reach))
        found = sum((place == last).astype(jnp.int32) for place in places)
        for side, jac in enumerate((jac_near, jac_far)):
            block = jac[base + j, chosen]
            aside[j, :, side * cells : (side + 1) * cells] = jnp.where(found > 0, block, jnp.zeros_like(block))


def gather_kernel(mine, other, out):
    half = mine.shape[0]

    def step(j, _):
        out[j] = mine[j]
        out[half + j] = other[j]
        return 0

    lax.fori_loop(0, half, step, 0)
    out[2 * half] = jnp.zeros(out.shape[1:], BF16)


def encode(value, out):
    width = value.shape[0]
    top = jnp.max(jnp.abs(value), axis=0, keepdims=True)
    power = jnp.clip(jnp.floor(jnp.log2(jnp.maximum(top, 1e-30))) + 1.0, -96.0, 96.0)
    coded = jnp.clip(jnp.round(value * jnp.exp2(15.0 - power)), -32767.0, 32767.0)
    out[:width] = coded.astype(jnp.int32).astype(jnp.int16)
    rows = jnp.broadcast_to(power.astype(jnp.int32), (PAD, power.shape[1]))
    out[width:] = rows.astype(jnp.int16)


def decode(part):
    width = part.shape[0] - PAD
    power = part[width:].astype(jnp.int32).astype(F32)[:1]
    return part[:width].astype(jnp.int32).astype(F32) * jnp.exp2(power - 15.0)


def late_kernel(cap, table, images, aside, jac_near, jac_far, near, far, noise, out, kept, sent):
    half, width, rows = out.shape
    slots, reach, _, cells = jac_near.shape
    base = core_index() * half
    at = len(OFFSETS) * (cap + 1) + base
    live = table[len(OFFSETS) * (cap + 1) + reach * slots]
    band = jnp.concatenate([near[...], far[...]], axis=0)
    size = half // 2
    for first in range(0, half, size):
        product = dot(jnp.concatenate([aside[first + j] for j in range(size)], axis=0), band)
        for j in range(size):
            slot = base + first + j
            scale = noise[pl.ds(slot, 1), :] * (slot < live).astype(F32)
            image = images[first + j] + product[j * rows : (j + 1) * rows]
            out[first + j] = (image.T * scale).astype(BF16)

    left = jnp.concatenate([out[j] for j in range(half)], axis=1)
    total = dot(left, jnp.concatenate([aside[j] for j in range(half)], axis=0))
    kept[0] = total[:, :cells]
    encode(total[:, cells:], sent.at[0])
    ahead = place_of("ahead")
    left, right = [], []
    for j in range(half):
        places = [table[at + f * slots + j] for f in range(reach)]
        chosen = sum(f * (places[f] == ahead).astype(jnp.int32) for f in range(reach))
        found = sum((place == ahead).astype(jnp.int32) for place in places)
        block = out[j]
        left.append(jnp.where(found > 0, block, jnp.zeros_like(block)))
        right.append(jnp.concatenate([jac_near[base + j, chosen], jac_far[base + j, chosen]], axis=1))
    total = dot(jnp.concatenate(left, axis=1), jnp.concatenate(right, axis=0))
    kept[1] = total[:, :cells]
    encode(total[:, cells:], sent.at[1])


def backward_kernel(roles, coded, cap, table, jac, weighted, *rest):
    outs, total = rest[:-1], rest[-1]
    slots = jac.shape[0]
    half = slots // 2
    counts = len(OFFSETS) * cap
    core = core_index()
    for role, code_it, out in zip(roles, coded, outs, strict=True):
        o = place_of(role)
        count = table[counts + o]

        def product(size):
            left, right = [], []
            for n in range(size):
                code = jnp.where(n < count, table[o * cap + n], slots * 4)
                j, f = lax.shift_right_logical(code, 2), jnp.bitwise_and(code, 3)
                left.append(weighted[j])
                right.append(jac[lax.rem(j + core * half, slots), f])
            total[...] = dot(jnp.concatenate(left, axis=1), jnp.concatenate(right, axis=0))

        below = -1
        for size in range(slots * 3 // 8, slots + 1, STEP):
            pl.when((count > below) & (count <= size))(functools.partial(product, size))
            below = size
        if code_it:
            encode(total[...], out)
        else:
            out[...] = total[...]


def merge_kernel(value, part, out):
    encode(value[...] + decode(part), out)


def merge_two_kernel(kept, sent, first, second):
    encode(kept[0] + decode(sent.at[0]), first)
    encode(kept[1] + decode(sent.at[1]), second)


def field_kernel(probes, own, *rest):
    parts, (field, keep, send) = rest[:3], rest[3:]
    width = own.shape[0]
    total = probes[...].astype(F32).T + own[...]
    for part in parts:
        total = total + decode(part)
    field[...] = total
    both = halves(total)
    gram = dot3(both, both, NT)
    mid, quarter = width // 2, width // 4
    first = core_index() == 0
    corner = gram[mid:, :mid]
    folded, ends = fold(gram[:mid, :mid], gram[mid:, mid:])
    low = jnp.concatenate([corner[:quarter], folded[:quarter], ends], axis=0)
    high = jnp.concatenate([corner[quarter:], folded[quarter:], ends], axis=0)
    keep[...] = jnp.where(first, low, high)
    send[...] = jnp.where(first, high, low)


def positions(square):
    row = lax.broadcasted_iota(jnp.int32, square.shape, 0)
    return row, lax.broadcasted_iota(jnp.int32, square.shape, 1)


def fold(lower, upper):
    row, column = positions(lower)
    diagonal = jnp.sum(jnp.where(row == column, upper, 0.0), axis=0, keepdims=True)
    return jnp.where(row >= column, lower, upper), jnp.broadcast_to(diagonal, (ROWS, lower.shape[1]))


def unfold(folded, ends):
    row, column = positions(folded)
    other = folded.T
    lower = jnp.where(row >= column, folded, other)
    upper = jnp.where(row < column, folded, other)
    return lower, jnp.where(row == column, ends[:1], upper)


def finish_kernel(scale, rounds, mine, other, field, basis, factor, gram, inverse, a_high, a_low):
    width = gram.shape[0]
    mid, quarter = width // 2, width // 4
    first = core_index() == 0
    low = jnp.where(first, mine[...], other[...])
    high = jnp.where(first, other[...], mine[...])
    folded = jnp.concatenate([low[quarter:mid], high[quarter:mid]], axis=0)
    gram[:mid, :mid], gram[mid:, mid:] = unfold(folded, low[mid:])
    corner = jnp.concatenate([low[:quarter], high[:quarter]], axis=0)
    gram[mid:, :mid] = corner
    gram[:mid, mid:] = corner.T
    matrix = gram[...]
    row = lax.broadcasted_iota(jnp.int32, matrix.shape, 0)
    column = lax.broadcasted_iota(jnp.int32, matrix.shape, 1)
    eye = (row == column).astype(F32)
    diagonal = matrix * eye
    down = lax.rsqrt(jnp.sum(diagonal, axis=1, keepdims=True))
    along = lax.rsqrt(jnp.sum(diagonal, axis=0, keepdims=True))
    unit = matrix * down * along
    parts = halves(unit)
    a_high[...], a_low[...] = parts

    def correction(error):
        return jnp.where(row > column, error, 0.5 * eye * error).astype(BF16)

    now = (eye - jnp.where(row > column, unit, 0.0)).astype(BF16)
    for _ in range(rounds):
        error = dot(dot(now, a_high[...]).astype(BF16), now, NT) - eye
        exact = now.astype(F32) - dot(correction(error), now)
        now = exact.astype(BF16)
    full = halves(exact)
    error = dot3(halves(dot3(full, (a_high[...], a_low[...]))), full, NT) - eye
    left = jnp.sum(error * error)
    solution_of = (exact - dot(correction(error), full[0])) * along
    inverse[...] = solution_of
    upper = dot3(halves(solution_of), halves(matrix)) * (1.0 / scale)
    factor[...] = jnp.where(row <= column, upper, 0.0)

    @pl.when(jnp.logical_not(left < 1e-2))
    def _():
        inverse[...] = eye
        across = lax.broadcasted_iota(jnp.int32, (1, width), 1)
        down_at = lax.broadcasted_iota(jnp.int32, (width, 1), 0)

        def eliminate(k, _):
            pivot_row = gram[pl.ds(k, 1), :]
            pivot = jnp.sum(jnp.where(across == k, pivot_row, 0.0), axis=1, keepdims=True)
            scaled = pivot_row * lax.rsqrt(pivot)
            now = gram[...]
            below = jnp.sum(jnp.where(column == k, now, 0.0), axis=1, keepdims=True)
            below = jnp.where(down_at > k, below * lax.rsqrt(pivot), 0.0)
            done = inverse[pl.ds(k, 1), :] * lax.rsqrt(pivot)
            factor[pl.ds(k, 1), :] = jnp.where(across >= k, scaled * (1.0 / scale), 0.0)
            gram[...] = now - below * scaled
            inverse[...] = inverse[...] - below * done
            inverse[pl.ds(k, 1), :] = done
            return 0

        lax.fori_loop(0, width, eliminate, 0)

    solved = halves(inverse[...])
    basis[...] = (dot3(solved, halves(field[...])) * scale).T


def all_reduced(value):
    count = lax.axis_size("tile")
    if count & (count - 1):
        return lax.psum(value, "tile")

    def exchanged(jump):
        return lax.ppermute(value, "tile", [(i, i ^ jump) for i in range(count)])

    bit = 1
    while bit < count:
        if bit == 1 or 2 * bit == count:
            value = value + exchanged(bit)
            bit *= 2
        else:
            first, second, third = exchanged(bit), exchanged(2 * bit), exchanged(3 * bit)
            value = (value + first) + (second + third)
            bit *= 4
    return value


def on_device(jacobian, footprint, live, noise_weight, probes):
    slots, reach, rows, cells = jacobian.shape
    width = probes.shape[2]
    half = slots // lax.axis_size("col")
    cap = slots
    mine = probes[0]

    back, ahead, partner = spread(mine, -2), spread(mine, 2), swapped(mine)
    jac_far = flipped(jacobian)
    staged = kernel_call(
        stage_kernel,
        pltpu.VMEM(jacobian.shape, BF16),
        [HBM],
        VMEM,
        [pltpu.SemaphoreType.DMA(())],
    )(held(jacobian, pltpu.HBM))
    back, staged = lax.optimization_barrier((back, staged))
    table = kernel_call(
        functools.partial(list_kernel, cap, half),
        pltpu.SMEM((len(OFFSETS) * (cap + 1) + reach * slots + 1,), jnp.int32),
        [SMEM] * 2,
        SMEM,
    )(footprint.T, live)
    near = [mine, back, ahead, partner]
    far = [flipped(mine), flipped(back)]
    ahead, partner, _, table = lax.optimization_barrier((ahead, partner, far[1], table))
    table = held(table, pltpu.SMEM)
    far += [flipped(ahead), flipped(partner)]

    early = kernel_call(
        functools.partial(early_kernel, cap),
        (
            jax.ShapeDtypeStruct((half, rows, width), F32),
            jax.ShapeDtypeStruct((half, rows, 2 * cells), BF16),
        ),
        [SMEM] + [VMEM] * 10,
        (VMEM,) * 2,
        [pltpu.VMEM((len(OFFSETS), 2 * cells, width), BF16)],
    )(table, held(staged, pltpu.VMEM), held(jac_far, pltpu.VMEM), *near, *far)
    beyond = swapped(back)
    plain = jax.ShapeDtypeStruct((width, cells), F32)
    message = jax.ShapeDtypeStruct((width + PAD, cells), jnp.int16)
    weighted, kept, sent = kernel_call(
        functools.partial(late_kernel, cap),
        (
            jax.ShapeDtypeStruct((half, width, rows), BF16),
            jax.ShapeDtypeStruct((2,) + plain.shape, F32),
            jax.ShapeDtypeStruct((2,) + message.shape, jnp.int16),
        ),
        [SMEM] + [VMEM] * 7,
        (VMEM,) * 3,
    )(table, *early, held(staged, pltpu.VMEM), held(jac_far, pltpu.VMEM), beyond, flipped(beyond), noise_weight)
    beyond, ahead = kernel_call(merge_two_kernel, (message, message), [VMEM] * 2, (VMEM,) * 2)(kept, flipped(sent))
    beyond, ahead, weighted = lax.optimization_barrier((beyond, ahead, weighted))
    beyond, ahead = swapped(beyond), spread(ahead, -2)
    weighted = kernel_call(
        gather_kernel,
        jax.ShapeDtypeStruct((2 * half + 1, width, rows), BF16),
        [VMEM] * 2,
        VMEM,
    )(weighted, flipped(weighted))

    def buckets(roles, coded, weighted):
        return kernel_call(
            functools.partial(backward_kernel, roles, coded, cap),
            [message if code_it else plain for code_it in coded],
            [SMEM] + [VMEM] * 2,
            [VMEM] * len(roles),
            [pltpu.VMEM((width, cells), F32)],
        )(table, held(staged, pltpu.VMEM), weighted)

    back, partner = buckets(("back", "partner"), (False, True), weighted)
    back = kernel_call(merge_kernel, message, [VMEM] * 2, VMEM)(back, beyond)
    back, partner, weighted = lax.optimization_barrier((back, partner, weighted))
    arrived = [spread(back, 2), ahead, swapped(partner)]
    own = buckets(("own",), (False,), weighted)[0]
    packed = jax.ShapeDtypeStruct((width // 2 + ROWS, width // 2), F32)
    field, keep, send = kernel_call(
        field_kernel,
        (plain, packed, packed),
        [VMEM] * 5,
        (VMEM,) * 3,
    )(mine, own, *arrived)
    summed = all_reduced(keep + flipped(send))
    scale = math.sqrt(cells * lax.axis_size("col") * lax.axis_size("tile"))
    square = jax.ShapeDtypeStruct((width, width), F32)
    basis, factor = kernel_call(
        functools.partial(finish_kernel, scale, 2),
        (jax.ShapeDtypeStruct((cells, width), F32), square),
        [VMEM] * 3,
        (VMEM,) * 2,
        [pltpu.VMEM((width, width), F32)] * 2 + [pltpu.VMEM((width, width), BF16)] * 2,
    )(summed, flipped(summed), field)
    return (basis[None], factor)


def solution(mesh):
    placed = (
        P(("groups", "tile"), None, None, "col"),
        P(("groups", "tile"), None),
        P(("groups", "tile")),
        P(("groups", "tile"), None),
        P(("groups", "tile"), "col", None),
    )
    return jax.shard_map(
        on_device,
        mesh=mesh,
        in_specs=placed,
        out_specs=(P(("groups", "tile"), "col", None), P("groups", None)),
        check_vma=False,
    )
```

```python
import functools
import math

import jax
import jax.numpy as jnp
from jax import lax
from jax.experimental import pallas as pl
from jax.experimental.pallas import tpu as pltpu
from jax.sharding import PartitionSpec as P

F32 = jnp.float32
BF16 = jnp.bfloat16
NN = (((1,), (0,)), ((), ()))
NT = (((1,), (1,)), ((), ()))
OFFSETS = (-2, -1, 0, 1, 2)
PAD = 16
ROWS = 8
LIMIT = 16 << 20
VMEM = pl.BlockSpec(memory_space=pltpu.VMEM)
SMEM = pl.BlockSpec(memory_space=pltpu.SMEM)
HBM = pl.BlockSpec(memory_space=pltpu.HBM)
STEP = 4


def kernel_call(body, out_shape, in_specs, out_specs, scratch=(), flops=1024, nbytes=1024):
    return pl.pallas_call(
        body,
        out_shape=out_shape,
        in_specs=in_specs,
        out_specs=out_specs,
        scratch_shapes=list(scratch),
        compiler_params=pltpu.CompilerParams(vmem_limit_bytes=LIMIT),
        cost_estimate=pl.CostEstimate(flops=flops, bytes_accessed=nbytes, transcendentals=0),
    )


def dot(a, b, dims=NN):
    return lax.dot_general(a, b, dims, preferred_element_type=F32)


def halves(a):
    high = a.astype(BF16)
    return high, (a - high.astype(F32)).astype(BF16)


def dot3(a, b, dims=NN):
    a_high, a_low = a
    b_high, b_low = b
    return dot(a_high, b_high, dims) + (dot(a_high, b_low, dims) + dot(a_low, b_high, dims))


held = pltpu.with_memory_space_constraint


def shifted(value, axis, steps):
    count = lax.axis_size(axis)
    pairs = [(source, (source + steps) % count) for source in range(count)]
    return lax.ppermute(value, axis, pairs)


def flipped(value):
    return shifted(value, "col", 1)


def swapped(value):
    return lax.ppermute(value, "tile", [(i, i ^ 1) for i in range(lax.axis_size("tile"))])


def spread(value, steps):
    count = lax.axis_size("tile")
    return lax.ppermute(value, "tile", [(i, (i + (steps, -steps)[i % 2]) % count) for i in range(count)])


ROLES = ("own", "back", "ahead", "partner", "beyond")


def core_index():
    return lax.axis_index("col").astype(jnp.int32)


def place_of(role):
    parity = lax.rem(lax.axis_index("tile").astype(jnp.int32), 2)
    return {
        "own": 2,
        "back": 4 - 4 * parity,
        "ahead": 4 * parity,
        "partner": 3 - 2 * parity,
        "beyond": 1 + 2 * parity,
    }[role]


def list_kernel(cap, half, footprint, live, table):
    reach, slots = footprint.shape
    core = core_index()
    counts = len(OFFSETS) * cap
    places = counts + len(OFFSETS)
    table[places + reach * slots] = live[0]
    for o in range(len(OFFSETS)):
        table[counts + o] = 0

    def step(j, _):
        slot = lax.rem(j + core * half, slots)
        alive = (slot < live[0]).astype(jnp.int32)
        for f in range(reach):
            o = footprint[f, slot]
            table[places + f * slots + slot] = o
            n = table[counts + o]
            table[o * cap + n] = j * 4 + f
            table[counts + o] = n + alive
        return 0

    lax.fori_loop(0, slots, step, 0)


def stage_kernel(value, out, sem):
    copy = pltpu.make_async_copy(value, out, sem)
    copy.start()
    copy.wait()


def early_kernel(cap, table, jac_near, jac_far, *rest):
    count = len(ROLES) - 1
    near, far = rest[:count], rest[count : 2 * count]
    images, aside, window = rest[2 * count :]
    slots = images.shape[0]
    total, reach, _, cells = jac_near.shape
    base = core_index() * slots
    at = len(OFFSETS) * (cap + 1) + base
    for i in range(count):
        o = place_of(ROLES[i])
        window[o, :cells] = near[i][...]
        window[o, cells:] = far[i][...]
    last = place_of(ROLES[count])
    window[last] = jnp.zeros(window.shape[1:], BF16)
    for j in range(slots):
        places = [table[at + f * total + j] for f in range(reach)]
        pieces = [jac[base + j, f] for f in range(reach) for jac in (jac_near, jac_far)]
        bands = [window[place] for place in places]
        images[j] = dot(jnp.concatenate(pieces, axis=1), jnp.concatenate(bands, axis=0))
        chosen = sum(f * (places[f] == last).astype(jnp.int32) for f in range(reach))
        found = sum((place == last).astype(jnp.int32) for place in places)
        for side, jac in enumerate((jac_near, jac_far)):
            block = jac[base + j, chosen]
            aside[j, :, side * cells : (side + 1) * cells] = jnp.where(found > 0, block, jnp.zeros_like(block))


def gather_kernel(mine, other, out):
    half = mine.shape[0]

    def step(j, _):
        out[j] = mine[j]
        out[half + j] = other[j]
        return 0

    lax.fori_loop(0, half, step, 0)
    out[2 * half] = jnp.zeros(out.shape[1:], BF16)


def encode(value, out):
    width = value.shape[0]
    top = jnp.max(jnp.abs(value), axis=0, keepdims=True)
    power = jnp.clip(jnp.floor(jnp.log2(jnp.maximum(top, 1e-30))) + 1.0, -96.0, 96.0)
    coded = jnp.clip(jnp.round(value * jnp.exp2(15.0 - power)), -32767.0, 32767.0)
    out[:width] = coded.astype(jnp.int32).astype(jnp.int16)
    rows = jnp.broadcast_to(power.astype(jnp.int32), (PAD, power.shape[1]))
    out[width:] = rows.astype(jnp.int16)


def decode(part):
    width = part.shape[0] - PAD
    power = part[width:].astype(jnp.int32).astype(F32)[:1]
    return part[:width].astype(jnp.int32).astype(F32) * jnp.exp2(power - 15.0)


def late_kernel(cap, table, images, aside, near, far, noise, out, kept, sent):
    half, width, rows = out.shape
    base = core_index() * half
    live = table[table.shape[0] - 1]
    band = jnp.concatenate([near[...], far[...]], axis=0)
    size = half // 2
    for first in range(0, half, size):
        product = dot(jnp.concatenate([aside[first + j] for j in range(size)], axis=0), band)
        for j in range(size):
            slot = base + first + j
            scale = noise[pl.ds(slot, 1), :] * (slot < live).astype(F32)
            image = images[first + j] + product[j * rows : (j + 1) * rows]
            out[first + j] = (image.T * scale).astype(BF16)

    left = jnp.concatenate([out[j] for j in range(half)], axis=1)
    put_bucket(dot(left, jnp.concatenate([aside[j] for j in range(half)], axis=0)), kept, sent)


def put_bucket(total, kept, sent):
    cells = kept.shape[1]
    kept[...] = total[:, :cells]
    encode(total[:, cells:], sent)


def ahead_kernel(cap, table, weighted, jac_near, jac_far, kept, sent):
    half = weighted.shape[0]
    slots, reach = jac_near.shape[:2]
    base = core_index() * half
    at = len(OFFSETS) * (cap + 1) + base
    wanted = place_of("ahead")
    left, right = [], []
    for j in range(half):
        places = [table[at + f * slots + j] for f in range(reach)]
        chosen = sum(f * (places[f] == wanted).astype(jnp.int32) for f in range(reach))
        found = sum((place == wanted).astype(jnp.int32) for place in places)
        block = weighted[j]
        left.append(jnp.where(found > 0, block, jnp.zeros_like(block)))
        right.append(jnp.concatenate([jac_near[base + j, chosen], jac_far[base + j, chosen]], axis=1))
    put_bucket(dot(jnp.concatenate(left, axis=1), jnp.concatenate(right, axis=0)), kept, sent)


def backward_kernel(roles, coded, cap, table, jac, weighted, *rest):
    outs, total = rest[:-1], rest[-1]
    slots = jac.shape[0]
    half = slots // 2
    counts = len(OFFSETS) * cap
    core = core_index()
    for role, code_it, out in zip(roles, coded, outs, strict=True):
        o = place_of(role)
        count = table[counts + o]

        def product(size):
            left, right = [], []
            for n in range(size):
                code = jnp.where(n < count, table[o * cap + n], slots * 4)
                j, f = lax.shift_right_logical(code, 2), jnp.bitwise_and(code, 3)
                left.append(weighted[j])
                right.append(jac[lax.rem(j + core * half, slots), f])
            total[...] = dot(jnp.concatenate(left, axis=1), jnp.concatenate(right, axis=0))

        below = -1
        for size in range(slots * 3 // 8, slots + 1, STEP):
            pl.when((count > below) & (count <= size))(functools.partial(product, size))
            below = size
        if code_it:
            encode(total[...], out)
        else:
            out[...] = total[...]


def merge_kernel(value, part, out):
    encode(value[...] + decode(part), out)


def field_kernel(probes, own, *rest):
    parts, (field, keep, send) = rest[:3], rest[3:]
    width = own.shape[0]
    total = probes[...].astype(F32).T + own[...]
    for part in parts:
        total = total + decode(part)
    field[...] = total
    both = halves(total)
    gram = dot3(both, both, NT)
    mid, quarter = width // 2, width // 4
    first = core_index() == 0
    corner = gram[mid:, :mid]
    folded, ends = fold(gram[:mid, :mid], gram[mid:, mid:])
    low = jnp.concatenate([corner[:quarter], folded[:quarter], ends], axis=0)
    high = jnp.concatenate([corner[quarter:], folded[quarter:], ends], axis=0)
    keep[...] = jnp.where(first, low, high)
    send[...] = jnp.where(first, high, low)


def positions(square):
    row = lax.broadcasted_iota(jnp.int32, square.shape, 0)
    return row, lax.broadcasted_iota(jnp.int32, square.shape, 1)


def fold(lower, upper):
    row, column = positions(lower)
    diagonal = jnp.sum(jnp.where(row == column, upper, 0.0), axis=0, keepdims=True)
    return jnp.where(row >= column, lower, upper), jnp.broadcast_to(diagonal, (ROWS, lower.shape[1]))


def unfold(folded, ends):
    row, column = positions(folded)
    other = folded.T
    lower = jnp.where(row >= column, folded, other)
    upper = jnp.where(row < column, folded, other)
    return lower, jnp.where(row == column, ends[:1], upper)


def finish_kernel(scale, rounds, mine, other, field, basis, factor, gram, inverse, a_high, a_low):
    width = gram.shape[0]
    mid, quarter = width // 2, width // 4
    first = core_index() == 0
    low = jnp.where(first, mine[...], other[...])
    high = jnp.where(first, other[...], mine[...])
    folded = jnp.concatenate([low[quarter:mid], high[quarter:mid]], axis=0)
    gram[:mid, :mid], gram[mid:, mid:] = unfold(folded, low[mid:])
    corner = jnp.concatenate([low[:quarter], high[:quarter]], axis=0)
    gram[mid:, :mid] = corner
    gram[:mid, mid:] = corner.T
    matrix = gram[...]
    row = lax.broadcasted_iota(jnp.int32, matrix.shape, 0)
    column = lax.broadcasted_iota(jnp.int32, matrix.shape, 1)
    eye = (row == column).astype(F32)
    diagonal = matrix * eye
    down = lax.rsqrt(jnp.sum(diagonal, axis=1, keepdims=True))
    along = lax.rsqrt(jnp.sum(diagonal, axis=0, keepdims=True))
    unit = matrix * down * along
    parts = halves(unit)
    a_high[...], a_low[...] = parts

    def correction(error):
        return jnp.where(row > column, error, 0.5 * eye * error).astype(BF16)

    now = (eye - jnp.where(row > column, unit, 0.0)).astype(BF16)
    for _ in range(rounds):
        error = dot(dot(now, a_high[...]).astype(BF16), now, NT) - eye
        exact = now.astype(F32) - dot(correction(error), now)
        now = exact.astype(BF16)
    full = halves(exact)
    error = dot3(halves(dot3(full, (a_high[...], a_low[...]))), full, NT) - eye
    left = jnp.sum(error * error)
    solution_of = (exact - dot(correction(error), full[0])) * along
    inverse[...] = solution_of
    upper = dot3(halves(solution_of), halves(matrix)) * (1.0 / scale)
    factor[...] = jnp.where(row <= column, upper, 0.0)

    @pl.when(jnp.logical_not(left < 1e-2))
    def _():
        inverse[...] = eye
        across = lax.broadcasted_iota(jnp.int32, (1, width), 1)
        down_at = lax.broadcasted_iota(jnp.int32, (width, 1), 0)

        def eliminate(k, _):
            pivot_row = gram[pl.ds(k, 1), :]
            pivot = jnp.sum(jnp.where(across == k, pivot_row, 0.0), axis=1, keepdims=True)
            scaled = pivot_row * lax.rsqrt(pivot)
            now = gram[...]
            below = jnp.sum(jnp.where(column == k, now, 0.0), axis=1, keepdims=True)
            below = jnp.where(down_at > k, below * lax.rsqrt(pivot), 0.0)
            done = inverse[pl.ds(k, 1), :] * lax.rsqrt(pivot)
            factor[pl.ds(k, 1), :] = jnp.where(across >= k, scaled * (1.0 / scale), 0.0)
            gram[...] = now - below * scaled
            inverse[...] = inverse[...] - below * done
            inverse[pl.ds(k, 1), :] = done
            return 0

        lax.fori_loop(0, width, eliminate, 0)

    solved = halves(inverse[...])
    basis[...] = (dot3(solved, halves(field[...])) * scale).T


def all_reduced(value):
    count = lax.axis_size("tile")
    if count & (count - 1):
        return lax.psum(value, "tile")

    def exchanged(jump):
        return lax.ppermute(value, "tile", [(i, i ^ jump) for i in range(count)])

    bit = 1
    while bit < count:
        if bit == 1 or 2 * bit == count:
            value = value + exchanged(bit)
            bit *= 2
        else:
            first, second, third = exchanged(bit), exchanged(2 * bit), exchanged(3 * bit)
            value = (value + first) + (second + third)
            bit *= 4
    return value


def on_device(jacobian, footprint, live, noise_weight, probes):
    slots, reach, rows, cells = jacobian.shape
    width = probes.shape[2]
    half = slots // lax.axis_size("col")
    cap = slots
    mine = probes[0]

    back, ahead, partner = spread(mine, -2), spread(mine, 2), swapped(mine)
    jac_far = flipped(jacobian)
    staged = kernel_call(
        stage_kernel,
        pltpu.VMEM(jacobian.shape, BF16),
        [HBM],
        VMEM,
        [pltpu.SemaphoreType.DMA(())],
    )(held(jacobian, pltpu.HBM))
    back, staged = lax.optimization_barrier((back, staged))
    table = kernel_call(
        functools.partial(list_kernel, cap, half),
        pltpu.SMEM((len(OFFSETS) * (cap + 1) + reach * slots + 1,), jnp.int32),
        [SMEM] * 2,
        SMEM,
    )(footprint.T, live)
    near = [mine, back, ahead, partner]
    far = [flipped(mine), flipped(back)]
    ahead, partner, _, table = lax.optimization_barrier((ahead, partner, far[1], table))
    table = held(table, pltpu.SMEM)
    far += [flipped(ahead), flipped(partner)]

    early = kernel_call(
        functools.partial(early_kernel, cap),
        (
            jax.ShapeDtypeStruct((half, rows, width), F32),
            jax.ShapeDtypeStruct((half, rows, 2 * cells), BF16),
        ),
        [SMEM] + [VMEM] * 10,
        (VMEM,) * 2,
        [pltpu.VMEM((len(OFFSETS), 2 * cells, width), BF16)],
    )(table, held(staged, pltpu.VMEM), held(jac_far, pltpu.VMEM), *near, *far)
    beyond = swapped(back)
    plain = jax.ShapeDtypeStruct((width, cells), F32)
    message = jax.ShapeDtypeStruct((width + PAD, cells), jnp.int16)
    shares = (held(staged, pltpu.VMEM), held(jac_far, pltpu.VMEM))
    weighted, kept, sent = kernel_call(
        functools.partial(late_kernel, cap),
        (jax.ShapeDtypeStruct((half, width, rows), BF16), plain, message),
        [SMEM] + [VMEM] * 5,
        (VMEM,) * 3,
    )(table, *early, beyond, flipped(beyond), noise_weight)
    kept_ahead, sent_ahead = kernel_call(
        functools.partial(ahead_kernel, cap),
        (plain, message),
        [SMEM] + [VMEM] * 3,
        (VMEM,) * 2,
    )(table, weighted, *shares)

    def merged(value, part):
        return kernel_call(merge_kernel, message, [VMEM] * 2, VMEM)(value, part)

    sent, sent_ahead = lax.optimization_barrier((flipped(sent), sent_ahead))
    beyond = merged(kept, sent)
    beyond, sent_ahead, weighted = lax.optimization_barrier((beyond, sent_ahead, weighted))
    beyond, ahead = swapped(beyond), spread(merged(kept_ahead, flipped(sent_ahead)), -2)
    weighted = kernel_call(
        gather_kernel,
        jax.ShapeDtypeStruct((2 * half + 1, width, rows), BF16),
        [VMEM] * 2,
        VMEM,
    )(weighted, flipped(weighted))

    def buckets(roles, coded, weighted):
        return kernel_call(
            functools.partial(backward_kernel, roles, coded, cap),
            [message if code_it else plain for code_it in coded],
            [SMEM] + [VMEM] * 2,
            [VMEM] * len(roles),
            [pltpu.VMEM((width, cells), F32)],
        )(table, held(staged, pltpu.VMEM), weighted)

    back, partner = buckets(("back", "partner"), (False, True), weighted)
    back = merged(back, beyond)
    back, partner, weighted = lax.optimization_barrier((back, partner, weighted))
    arrived = [spread(back, 2), ahead, swapped(partner)]
    own = buckets(("own",), (False,), weighted)[0]
    packed = jax.ShapeDtypeStruct((width // 2 + ROWS, width // 2), F32)
    field, keep, send = kernel_call(
        field_kernel,
        (plain, packed, packed),
        [VMEM] * 5,
        (VMEM,) * 3,
    )(mine, own, *arrived)
    summed = all_reduced(keep + flipped(send))
    scale = math.sqrt(cells * lax.axis_size("col") * lax.axis_size("tile"))
    square = jax.ShapeDtypeStruct((width, width), F32)
    basis, factor = kernel_call(
        functools.partial(finish_kernel, scale, 2),
        (jax.ShapeDtypeStruct((cells, width), F32), square),
        [VMEM] * 3,
        (VMEM,) * 2,
        [pltpu.VMEM((width, width), F32)] * 2 + [pltpu.VMEM((width, width), BF16)] * 2,
    )(summed, flipped(summed), field)
    return (basis[None], factor)


def solution(mesh):
    placed = (
        P(("groups", "tile"), None, None, "col"),
        P(("groups", "tile"), None),
        P(("groups", "tile")),
        P(("groups", "tile"), None),
        P(("groups", "tile"), "col", None),
    )
    return jax.shard_map(
        on_device,
        mesh=mesh,
        in_specs=placed,
        out_specs=(P(("groups", "tile"), "col", None), P("groups", None)),
        check_vma=False,
    )
```

```python
import functools
import math

import jax
import jax.numpy as jnp
from jax import lax
from jax.experimental import pallas as pl
from jax.experimental.pallas import tpu as pltpu
from jax.sharding import PartitionSpec as P

F32 = jnp.float32
BF16 = jnp.bfloat16
NN = (((1,), (0,)), ((), ()))
NT = (((1,), (1,)), ((), ()))
OFFSETS = (-2, -1, 0, 1, 2)
PAD = 16
ENOUGH = 1e-2
REFINED = 6
ROWS = 8
LIMIT = 16 << 20
VMEM = pl.BlockSpec(memory_space=pltpu.VMEM)
SMEM = pl.BlockSpec(memory_space=pltpu.SMEM)
HBM = pl.BlockSpec(memory_space=pltpu.HBM)
STEP = 4


def kernel_call(body, out_shape, in_specs, out_specs, scratch=(), flops=1024, nbytes=1024):
    return pl.pallas_call(
        body,
        out_shape=out_shape,
        in_specs=in_specs,
        out_specs=out_specs,
        scratch_shapes=list(scratch),
        compiler_params=pltpu.CompilerParams(vmem_limit_bytes=LIMIT),
        cost_estimate=pl.CostEstimate(flops=flops, bytes_accessed=nbytes, transcendentals=0),
    )


def dot(a, b, dims=NN):
    return lax.dot_general(a, b, dims, preferred_element_type=F32)


def halves(a):
    high = a.astype(BF16)
    return high, (a - high.astype(F32)).astype(BF16)


def dot3(a, b, dims=NN):
    a_high, a_low = a
    b_high, b_low = b
    return dot(a_high, b_high, dims) + (dot(a_high, b_low, dims) + dot(a_low, b_high, dims))


held = pltpu.with_memory_space_constraint


def shifted(value, axis, steps):
    count = lax.axis_size(axis)
    pairs = [(source, (source + steps) % count) for source in range(count)]
    return lax.ppermute(value, axis, pairs)


def flipped(value):
    return shifted(value, "col", 1)


def swapped(value):
    return lax.ppermute(value, "tile", [(i, i ^ 1) for i in range(lax.axis_size("tile"))])


def spread(value, steps):
    count = lax.axis_size("tile")
    return lax.ppermute(value, "tile", [(i, (i + (steps, -steps)[i % 2]) % count) for i in range(count)])


ROLES = ("own", "back", "ahead", "partner", "beyond")


def core_index():
    return lax.axis_index("col").astype(jnp.int32)


def place_of(role):
    parity = lax.rem(lax.axis_index("tile").astype(jnp.int32), 2)
    return {
        "own": 2,
        "back": 4 - 4 * parity,
        "ahead": 4 * parity,
        "partner": 3 - 2 * parity,
        "beyond": 1 + 2 * parity,
    }[role]


def list_kernel(cap, half, footprint, live, table):
    reach, slots = footprint.shape
    core = core_index()
    counts = len(OFFSETS) * cap
    places = counts + len(OFFSETS)
    table[places + reach * slots] = live[0]
    for o in range(len(OFFSETS)):
        table[counts + o] = 0

    def step(j, _):
        slot = lax.rem(j + core * half, slots)
        alive = (slot < live[0]).astype(jnp.int32)
        for f in range(reach):
            o = footprint[f, slot]
            table[places + f * slots + slot] = o
            n = table[counts + o]
            table[o * cap + n] = j * 4 + f
            table[counts + o] = n + alive
        return 0

    lax.fori_loop(0, slots, step, 0)


def stage_kernel(value, out, sem):
    copy = pltpu.make_async_copy(value, out, sem)
    copy.start()
    copy.wait()


def early_kernel(cap, table, jac_near, jac_far, *rest):
    count = len(ROLES) - 1
    near, far = rest[:count], rest[count : 2 * count]
    images, aside, window = rest[2 * count :]
    slots = images.shape[0]
    total, reach, _, cells = jac_near.shape
    base = core_index() * slots
    at = len(OFFSETS) * (cap + 1) + base
    for i in range(count):
        o = place_of(ROLES[i])
        window[o, :cells] = near[i][...]
        window[o, cells:] = far[i][...]
    last = place_of(ROLES[count])
    window[last] = jnp.zeros(window.shape[1:], BF16)
    for j in range(slots):
        places = [table[at + f * total + j] for f in range(reach)]
        pieces = [jac[base + j, f] for f in range(reach) for jac in (jac_near, jac_far)]
        bands = [window[place] for place in places]
        images[j] = dot(jnp.concatenate(pieces, axis=1), jnp.concatenate(bands, axis=0))
        chosen = sum(f * (places[f] == last).astype(jnp.int32) for f in range(reach))
        found = sum((place == last).astype(jnp.int32) for place in places)
        for side, jac in enumerate((jac_near, jac_far)):
            block = jac[base + j, chosen]
            aside[j, :, side * cells : (side + 1) * cells] = jnp.where(found > 0, block, jnp.zeros_like(block))


def gather_kernel(mine, other, out):
    half = mine.shape[0]

    def step(j, _):
        out[j] = mine[j]
        out[half + j] = other[j]
        return 0

    lax.fori_loop(0, half, step, 0)
    out[2 * half] = jnp.zeros(out.shape[1:], BF16)


def encode(value, out):
    width = value.shape[0]
    top = jnp.max(jnp.abs(value), axis=0, keepdims=True)
    power = jnp.clip(jnp.floor(jnp.log2(jnp.maximum(top, 1e-30))) + 1.0, -96.0, 96.0)
    coded = jnp.clip(jnp.round(value * jnp.exp2(15.0 - power)), -32767.0, 32767.0)
    out[:width] = coded.astype(jnp.int32).astype(jnp.int16)
    rows = jnp.broadcast_to(power.astype(jnp.int32), (PAD, power.shape[1]))
    out[width:] = rows.astype(jnp.int16)


def decode(part):
    width = part.shape[0] - PAD
    power = part[width:].astype(jnp.int32).astype(F32)[:1]
    return part[:width].astype(jnp.int32).astype(F32) * jnp.exp2(power - 15.0)


def late_kernel(cap, table, images, aside, near, far, noise, out, kept, sent):
    half, width, rows = out.shape
    base = core_index() * half
    live = table[table.shape[0] - 1]
    band = jnp.concatenate([near[...], far[...]], axis=0)
    size = half // 2
    for first in range(0, half, size):
        product = dot(jnp.concatenate([aside[first + j] for j in range(size)], axis=0), band)
        for j in range(size):
            slot = base + first + j
            scale = noise[pl.ds(slot, 1), :] * (slot < live).astype(F32)
            image = images[first + j] + product[j * rows : (j + 1) * rows]
            out[first + j] = (image.T * scale).astype(BF16)

    left = jnp.concatenate([out[j] for j in range(half)], axis=1)
    put_bucket(dot(left, jnp.concatenate([aside[j] for j in range(half)], axis=0)), kept, sent)


def put_bucket(total, kept, sent):
    cells = kept.shape[1]
    kept[...] = total[:, :cells]
    encode(total[:, cells:], sent)


def ahead_kernel(cap, table, weighted, jac_near, jac_far, kept, sent):
    half = weighted.shape[0]
    slots, reach = jac_near.shape[:2]
    base = core_index() * half
    at = len(OFFSETS) * (cap + 1) + base
    wanted = place_of("ahead")
    left, right = [], []
    for j in range(half):
        places = [table[at + f * slots + j] for f in range(reach)]
        chosen = sum(f * (places[f] == wanted).astype(jnp.int32) for f in range(reach))
        found = sum((place == wanted).astype(jnp.int32) for place in places)
        block = weighted[j]
        left.append(jnp.where(found > 0, block, jnp.zeros_like(block)))
        right.append(jnp.concatenate([jac_near[base + j, chosen], jac_far[base + j, chosen]], axis=1))
    put_bucket(dot(jnp.concatenate(left, axis=1), jnp.concatenate(right, axis=0)), kept, sent)


def backward_kernel(roles, coded, cap, table, jac, weighted, *rest):
    outs, total = rest[:-1], rest[-1]
    slots = jac.shape[0]
    half = slots // 2
    counts = len(OFFSETS) * cap
    core = core_index()
    for role, code_it, out in zip(roles, coded, outs, strict=True):
        o = place_of(role)
        count = table[counts + o]

        def product(size):
            left, right = [], []
            for n in range(size):
                code = jnp.where(n < count, table[o * cap + n], slots * 4)
                j, f = lax.shift_right_logical(code, 2), jnp.bitwise_and(code, 3)
                left.append(weighted[j])
                right.append(jac[lax.rem(j + core * half, slots), f])
            total[...] = dot(jnp.concatenate(left, axis=1), jnp.concatenate(right, axis=0))

        below = -1
        for size in range(slots * 3 // 8, slots + 1, STEP):
            pl.when((count > below) & (count <= size))(functools.partial(product, size))
            below = size
        if code_it:
            encode(total[...], out)
        else:
            out[...] = total[...]


def merge_kernel(value, part, out):
    encode(value[...] + decode(part), out)


def field_kernel(probes, own, *rest):
    parts, (field, keep, send) = rest[:3], rest[3:]
    width = own.shape[0]
    total = probes[...].astype(F32).T + own[...]
    for part in parts:
        total = total + decode(part)
    field[...] = total
    both = halves(total)
    gram = dot3(both, both, NT)
    mid, quarter = width // 2, width // 4
    first = core_index() == 0
    corner = gram[mid:, :mid]
    folded, ends = fold(gram[:mid, :mid], gram[mid:, mid:])
    low = jnp.concatenate([corner[:quarter], folded[:quarter], ends], axis=0)
    high = jnp.concatenate([corner[quarter:], folded[quarter:], ends], axis=0)
    keep[...] = jnp.where(first, low, high)
    send[...] = jnp.where(first, high, low)


def positions(square):
    row = lax.broadcasted_iota(jnp.int32, square.shape, 0)
    return row, lax.broadcasted_iota(jnp.int32, square.shape, 1)


def fold(lower, upper):
    row, column = positions(lower)
    diagonal = jnp.sum(jnp.where(row == column, upper, 0.0), axis=0, keepdims=True)
    return jnp.where(row >= column, lower, upper), jnp.broadcast_to(diagonal, (ROWS, lower.shape[1]))


def unfold(folded, ends):
    row, column = positions(folded)
    other = folded.T
    lower = jnp.where(row >= column, folded, other)
    upper = jnp.where(row < column, folded, other)
    return lower, jnp.where(row == column, ends[:1], upper)


def finish_kernel(scale, rounds, mine, other, field, basis, factor, gram, inverse, a_high, a_low):
    width = gram.shape[0]
    mid, quarter = width // 2, width // 4
    first = core_index() == 0
    low = jnp.where(first, mine[...], other[...])
    high = jnp.where(first, other[...], mine[...])
    folded = jnp.concatenate([low[quarter:mid], high[quarter:mid]], axis=0)
    gram[:mid, :mid], gram[mid:, mid:] = unfold(folded, low[mid:])
    corner = jnp.concatenate([low[:quarter], high[:quarter]], axis=0)
    gram[mid:, :mid] = corner
    gram[:mid, mid:] = corner.T
    matrix = gram[...]
    row = lax.broadcasted_iota(jnp.int32, matrix.shape, 0)
    column = lax.broadcasted_iota(jnp.int32, matrix.shape, 1)
    eye = (row == column).astype(F32)
    diagonal = matrix * eye
    down = lax.rsqrt(jnp.sum(diagonal, axis=1, keepdims=True))
    along = lax.rsqrt(jnp.sum(diagonal, axis=0, keepdims=True))
    unit = matrix * down * along
    parts = halves(unit)
    a_high[...], a_low[...] = parts

    def correction(error):
        return jnp.where(row > column, error, 0.5 * eye * error).astype(BF16)

    now = (eye - jnp.where(row > column, unit, 0.0)).astype(BF16)
    for _ in range(rounds):
        error = dot(dot(now, a_high[...]).astype(BF16), now, NT) - eye
        exact = now.astype(F32) - dot(correction(error), now)
        now = exact.astype(BF16)
    inverse[...] = exact

    def refined(state):
        full = halves(inverse[...])
        error = dot3(halves(dot3(full, (a_high[...], a_low[...]))), full, NT) - eye
        inverse[...] = inverse[...] - dot(correction(error), full[0])
        return state[0] + 1, jnp.sum(error * error)

    first = refined((0, 0.0))
    _, left = lax.while_loop(lambda state: (state[0] < REFINED) & (state[1] >= ENOUGH), refined, first)
    solution_of = inverse[...] * along
    inverse[...] = solution_of
    upper = dot3(halves(solution_of), halves(matrix)) * (1.0 / scale)
    factor[...] = jnp.where(row <= column, upper, 0.0)

    @pl.when(jnp.logical_not(left < ENOUGH))
    def _():
        inverse[...] = eye
        across = lax.broadcasted_iota(jnp.int32, (1, width), 1)
        down_at = lax.broadcasted_iota(jnp.int32, (width, 1), 0)

        def eliminate(k, _):
            pivot_row = gram[pl.ds(k, 1), :]
            pivot = jnp.sum(jnp.where(across == k, pivot_row, 0.0), axis=1, keepdims=True)
            scaled = pivot_row * lax.rsqrt(pivot)
            now = gram[...]
            below = jnp.sum(jnp.where(column == k, now, 0.0), axis=1, keepdims=True)
            below = jnp.where(down_at > k, below * lax.rsqrt(pivot), 0.0)
            done = inverse[pl.ds(k, 1), :] * lax.rsqrt(pivot)
            factor[pl.ds(k, 1), :] = jnp.where(across >= k, scaled * (1.0 / scale), 0.0)
            gram[...] = now - below * scaled
            inverse[...] = inverse[...] - below * done
            inverse[pl.ds(k, 1), :] = done
            return 0

        lax.fori_loop(0, width, eliminate, 0)

    solved = halves(inverse[...])
    basis[...] = (dot3(solved, halves(field[...])) * scale).T


def all_reduced(value):
    count = lax.axis_size("tile")
    if count & (count - 1):
        return lax.psum(value, "tile")

    def exchanged(jump):
        return lax.ppermute(value, "tile", [(i, i ^ jump) for i in range(count)])

    bit = 1
    while bit < count:
        if bit == 1 or 2 * bit == count:
            value = value + exchanged(bit)
            bit *= 2
        else:
            first, second, third = exchanged(bit), exchanged(2 * bit), exchanged(3 * bit)
            value = (value + first) + (second + third)
            bit *= 4
    return value


def on_device(jacobian, footprint, live, noise_weight, probes):
    slots, reach, rows, cells = jacobian.shape
    width = probes.shape[2]
    half = slots // lax.axis_size("col")
    cap = slots
    mine = probes[0]

    back, ahead, partner = spread(mine, -2), spread(mine, 2), swapped(mine)
    jac_far = flipped(jacobian)
    staged = kernel_call(
        stage_kernel,
        pltpu.VMEM(jacobian.shape, BF16),
        [HBM],
        VMEM,
        [pltpu.SemaphoreType.DMA(())],
    )(held(jacobian, pltpu.HBM))
    back, staged = lax.optimization_barrier((back, staged))
    table = kernel_call(
        functools.partial(list_kernel, cap, half),
        pltpu.SMEM((len(OFFSETS) * (cap + 1) + reach * slots + 1,), jnp.int32),
        [SMEM] * 2,
        SMEM,
    )(footprint.T, live)
    near = [mine, back, ahead, partner]
    far = [flipped(mine), flipped(back)]
    ahead, partner, _, table = lax.optimization_barrier((ahead, partner, far[1], table))
    table = held(table, pltpu.SMEM)
    far += [flipped(ahead), flipped(partner)]

    early = kernel_call(
        functools.partial(early_kernel, cap),
        (
            jax.ShapeDtypeStruct((half, rows, width), F32),
            jax.ShapeDtypeStruct((half, rows, 2 * cells), BF16),
        ),
        [SMEM] + [VMEM] * 10,
        (VMEM,) * 2,
        [pltpu.VMEM((len(OFFSETS), 2 * cells, width), BF16)],
    )(table, held(staged, pltpu.VMEM), held(jac_far, pltpu.VMEM), *near, *far)
    beyond = swapped(back)
    plain = jax.ShapeDtypeStruct((width, cells), F32)
    message = jax.ShapeDtypeStruct((width + PAD, cells), jnp.int16)
    shares = (held(staged, pltpu.VMEM), held(jac_far, pltpu.VMEM))
    weighted, kept, sent = kernel_call(
        functools.partial(late_kernel, cap),
        (jax.ShapeDtypeStruct((half, width, rows), BF16), plain, message),
        [SMEM] + [VMEM] * 5,
        (VMEM,) * 3,
    )(table, *early, beyond, flipped(beyond), noise_weight)
    kept_ahead, sent_ahead = kernel_call(
        functools.partial(ahead_kernel, cap),
        (plain, message),
        [SMEM] + [VMEM] * 3,
        (VMEM,) * 2,
    )(table, weighted, *shares)

    def merged(value, part):
        return kernel_call(merge_kernel, message, [VMEM] * 2, VMEM)(value, part)

    sent, sent_ahead = lax.optimization_barrier((flipped(sent), sent_ahead))
    beyond = merged(kept, sent)
    beyond, sent_ahead, weighted = lax.optimization_barrier((beyond, sent_ahead, weighted))
    beyond, ahead = swapped(beyond), spread(merged(kept_ahead, flipped(sent_ahead)), -2)
    weighted = kernel_call(
        gather_kernel,
        jax.ShapeDtypeStruct((2 * half + 1, width, rows), BF16),
        [VMEM] * 2,
        VMEM,
    )(weighted, flipped(weighted))

    def buckets(roles, coded, weighted):
        return kernel_call(
            functools.partial(backward_kernel, roles, coded, cap),
            [message if code_it else plain for code_it in coded],
            [SMEM] + [VMEM] * 2,
            [VMEM] * len(roles),
            [pltpu.VMEM((width, cells), F32)],
        )(table, held(staged, pltpu.VMEM), weighted)

    back, partner = buckets(("back", "partner"), (False, True), weighted)
    back = merged(back, beyond)
    back, partner, weighted = lax.optimization_barrier((back, partner, weighted))
    arrived = [spread(back, 2), ahead, swapped(partner)]
    own = buckets(("own",), (False,), weighted)[0]
    packed = jax.ShapeDtypeStruct((width // 2 + ROWS, width // 2), F32)
    field, keep, send = kernel_call(
        field_kernel,
        (plain, packed, packed),
        [VMEM] * 5,
        (VMEM,) * 3,
    )(mine, own, *arrived)
    summed = all_reduced(keep + flipped(send))
    scale = math.sqrt(cells * lax.axis_size("col") * lax.axis_size("tile"))
    square = jax.ShapeDtypeStruct((width, width), F32)
    basis, factor = kernel_call(
        functools.partial(finish_kernel, scale, 2),
        (jax.ShapeDtypeStruct((cells, width), F32), square),
        [VMEM] * 3,
        (VMEM,) * 2,
        [pltpu.VMEM((width, width), F32)] * 2 + [pltpu.VMEM((width, width), BF16)] * 2,
    )(summed, flipped(summed), field)
    return (basis[None], factor)


def solution(mesh):
    placed = (
        P(("groups", "tile"), None, None, "col"),
        P(("groups", "tile"), None),
        P(("groups", "tile")),
        P(("groups", "tile"), None),
        P(("groups", "tile"), "col", None),
    )
    return jax.shard_map(
        on_device,
        mesh=mesh,
        in_specs=placed,
        out_specs=(P(("groups", "tile"), "col", None), P("groups", None)),
        check_vma=False,
    )
```

```python
import functools
import math

import jax
import jax.numpy as jnp
from jax import lax
from jax.experimental import pallas as pl
from jax.experimental.pallas import tpu as pltpu
from jax.sharding import PartitionSpec as P

F32 = jnp.float32
BF16 = jnp.bfloat16
NN = (((1,), (0,)), ((), ()))
NT = (((1,), (1,)), ((), ()))
OFFSETS = (-2, -1, 0, 1, 2)
PAD = 16
ENOUGH = 1e-2
REFINED = 6
ROWS = 8
LIMIT = 16 << 20
VMEM = pl.BlockSpec(memory_space=pltpu.VMEM)
SMEM = pl.BlockSpec(memory_space=pltpu.SMEM)
HBM = pl.BlockSpec(memory_space=pltpu.HBM)
STEP = 4


def kernel_call(body, out_shape, in_specs, out_specs, scratch=(), flops=1024, nbytes=1024):
    return pl.pallas_call(
        body,
        out_shape=out_shape,
        in_specs=in_specs,
        out_specs=out_specs,
        scratch_shapes=list(scratch),
        compiler_params=pltpu.CompilerParams(vmem_limit_bytes=LIMIT),
        cost_estimate=pl.CostEstimate(flops=flops, bytes_accessed=nbytes, transcendentals=0),
    )


def dot(a, b, dims=NN):
    return lax.dot_general(a, b, dims, preferred_element_type=F32)


def halves(a):
    high = a.astype(BF16)
    return high, (a - high.astype(F32)).astype(BF16)


def dot3(a, b, dims=NN):
    a_high, a_low = a
    b_high, b_low = b
    return dot(a_high, b_high, dims) + (dot(a_high, b_low, dims) + dot(a_low, b_high, dims))


held = pltpu.with_memory_space_constraint


def shifted(value, axis, steps):
    count = lax.axis_size(axis)
    pairs = [(source, (source + steps) % count) for source in range(count)]
    return lax.ppermute(value, axis, pairs)


def flipped(value):
    return shifted(value, "col", 1)


def swapped(value):
    return lax.ppermute(value, "tile", [(i, i ^ 1) for i in range(lax.axis_size("tile"))])


def spread(value, steps):
    count = lax.axis_size("tile")
    return lax.ppermute(value, "tile", [(i, (i + (steps, -steps)[i % 2]) % count) for i in range(count)])


ROLES = ("own", "back", "ahead", "partner", "beyond")


def core_index():
    return lax.axis_index("col").astype(jnp.int32)


def place_of(role):
    parity = lax.rem(lax.axis_index("tile").astype(jnp.int32), 2)
    return {
        "own": 2,
        "back": 4 - 4 * parity,
        "ahead": 4 * parity,
        "partner": 3 - 2 * parity,
        "beyond": 1 + 2 * parity,
    }[role]


def list_kernel(cap, half, footprint, live, table):
    reach, slots = footprint.shape
    core = core_index()
    counts = len(OFFSETS) * cap
    places = counts + len(OFFSETS)
    table[places + reach * slots] = live[0]
    for o in range(len(OFFSETS)):
        table[counts + o] = 0

    def step(j, _):
        slot = lax.rem(j + core * half, slots)
        alive = (slot < live[0]).astype(jnp.int32)
        for f in range(reach):
            o = footprint[f, slot]
            table[places + f * slots + slot] = o
            n = table[counts + o]
            table[o * cap + n] = j * 4 + f
            table[counts + o] = n + alive
        return 0

    lax.fori_loop(0, slots, step, 0)


def stage_kernel(value, out, sem):
    copy = pltpu.make_async_copy(value, out, sem)
    copy.start()
    copy.wait()


def early_kernel(cap, table, jac_near, jac_far, *rest):
    count = len(ROLES) - 1
    near, far = rest[:count], rest[count : 2 * count]
    images, aside, window = rest[2 * count :]
    slots = images.shape[0]
    total, reach, _, cells = jac_near.shape
    base = core_index() * slots
    at = len(OFFSETS) * (cap + 1) + base
    for i in range(count):
        o = place_of(ROLES[i])
        window[o, :cells] = near[i][...]
        window[o, cells:] = far[i][...]
    last = place_of(ROLES[count])
    window[last] = jnp.zeros(window.shape[1:], BF16)
    for j in range(slots):
        places = [table[at + f * total + j] for f in range(reach)]
        pieces = [jac[base + j, f] for f in range(reach) for jac in (jac_near, jac_far)]
        bands = [window[place] for place in places]
        images[j] = dot(jnp.concatenate(pieces, axis=1), jnp.concatenate(bands, axis=0))
        chosen = sum(f * (places[f] == last).astype(jnp.int32) for f in range(reach))
        found = sum((place == last).astype(jnp.int32) for place in places)
        for side, jac in enumerate((jac_near, jac_far)):
            block = jac[base + j, chosen]
            aside[j, :, side * cells : (side + 1) * cells] = jnp.where(found > 0, block, jnp.zeros_like(block))


def gather_kernel(mine, other, out):
    half = mine.shape[0]

    def step(j, _):
        out[j] = mine[j]
        out[half + j] = other[j]
        return 0

    lax.fori_loop(0, half, step, 0)
    out[2 * half] = jnp.zeros(out.shape[1:], BF16)


def encode(value, out):
    width = value.shape[0]
    top = jnp.max(jnp.abs(value), axis=0, keepdims=True)
    power = jnp.clip(jnp.floor(jnp.log2(jnp.maximum(top, 1e-30))) + 1.0, -96.0, 96.0)
    coded = jnp.clip(jnp.round(value * jnp.exp2(15.0 - power)), -32767.0, 32767.0)
    out[:width] = coded.astype(jnp.int32).astype(jnp.int16)
    rows = jnp.broadcast_to(power.astype(jnp.int32), (PAD, power.shape[1]))
    out[width:] = rows.astype(jnp.int16)


def decode(part):
    width = part.shape[0] - PAD
    power = part[width:].astype(jnp.int32).astype(F32)[:1]
    return part[:width].astype(jnp.int32).astype(F32) * jnp.exp2(power - 15.0)


def late_kernel(cap, table, images, aside, near, far, noise, out, kept, sent):
    half, width, rows = out.shape
    base = core_index() * half
    live = table[table.shape[0] - 1]
    band = jnp.concatenate([near[...], far[...]], axis=0)
    size = half // 2
    for first in range(0, half, size):
        product = dot(jnp.concatenate([aside[first + j] for j in range(size)], axis=0), band)
        for j in range(size):
            slot = base + first + j
            scale = noise[pl.ds(slot, 1), :] * (slot < live).astype(F32)
            image = images[first + j] + product[j * rows : (j + 1) * rows]
            out[first + j] = (image.T * scale).astype(BF16)

    left = jnp.concatenate([out[j] for j in range(half)], axis=1)
    put_bucket(dot(left, jnp.concatenate([aside[j] for j in range(half)], axis=0)), kept, sent)


def put_bucket(total, kept, sent):
    cells = kept.shape[1]
    kept[...] = total[:, :cells]
    encode(total[:, cells:], sent)


def ahead_kernel(cap, table, weighted, jac_near, jac_far, kept, sent):
    half = weighted.shape[0]
    slots, reach = jac_near.shape[:2]
    base = core_index() * half
    at = len(OFFSETS) * (cap + 1) + base
    wanted = place_of("ahead")
    left, right = [], []
    for j in range(half):
        places = [table[at + f * slots + j] for f in range(reach)]
        chosen = sum(f * (places[f] == wanted).astype(jnp.int32) for f in range(reach))
        found = sum((place == wanted).astype(jnp.int32) for place in places)
        block = weighted[j]
        left.append(jnp.where(found > 0, block, jnp.zeros_like(block)))
        right.append(jnp.concatenate([jac_near[base + j, chosen], jac_far[base + j, chosen]], axis=1))
    put_bucket(dot(jnp.concatenate(left, axis=1), jnp.concatenate(right, axis=0)), kept, sent)


def backward_kernel(roles, coded, cap, table, jac, weighted, *rest):
    outs, total = rest[:-1], rest[-1]
    slots = jac.shape[0]
    half = slots // 2
    counts = len(OFFSETS) * cap
    core = core_index()
    for role, code_it, out in zip(roles, coded, outs, strict=True):
        o = place_of(role)
        count = table[counts + o]

        def product(size):
            left, right = [], []
            for n in range(size):
                code = jnp.where(n < count, table[o * cap + n], slots * 4)
                j, f = lax.shift_right_logical(code, 2), jnp.bitwise_and(code, 3)
                left.append(weighted[j])
                right.append(jac[lax.rem(j + core * half, slots), f])
            total[...] = dot(jnp.concatenate(left, axis=1), jnp.concatenate(right, axis=0))

        below = -1
        for size in range(slots * 3 // 8, slots + 1, STEP):
            pl.when((count > below) & (count <= size))(functools.partial(product, size))
            below = size
        if code_it:
            encode(total[...], out)
        else:
            out[...] = total[...]


def merge_kernel(value, part, out):
    encode(value[...] + decode(part), out)


def field_kernel(probes, own, *rest):
    parts, (field, keep, send) = rest[:3], rest[3:]
    width = own.shape[0]
    total = probes[...].astype(F32).T + own[...]
    for part in parts:
        total = total + decode(part)
    field[...] = total
    both = halves(total)
    gram = dot3(both, both, NT)
    mid, quarter = width // 2, width // 4
    first = core_index() == 0
    corner = gram[mid:, :mid]
    folded, ends = fold(gram[:mid, :mid], gram[mid:, mid:])
    low = jnp.concatenate([corner[:quarter], folded[:quarter], ends], axis=0)
    high = jnp.concatenate([corner[quarter:], folded[quarter:], ends], axis=0)
    keep[...] = jnp.where(first, low, high)
    send[...] = jnp.where(first, high, low)


def positions(square):
    row = lax.broadcasted_iota(jnp.int32, square.shape, 0)
    return row, lax.broadcasted_iota(jnp.int32, square.shape, 1)


def fold(lower, upper):
    row, column = positions(lower)
    diagonal = jnp.sum(jnp.where(row == column, upper, 0.0), axis=0, keepdims=True)
    return jnp.where(row >= column, lower, upper), jnp.broadcast_to(diagonal, (ROWS, lower.shape[1]))


def unfold(folded, ends):
    row, column = positions(folded)
    other = folded.T
    lower = jnp.where(row >= column, folded, other)
    upper = jnp.where(row < column, folded, other)
    return lower, jnp.where(row == column, ends[:1], upper)


def finish_kernel(scale, rounds, mine, other, field, basis, factor, gram, inverse, a_high, a_low):
    width = gram.shape[0]
    mid, quarter = width // 2, width // 4
    first = core_index() == 0
    low = jnp.where(first, mine[...], other[...])
    high = jnp.where(first, other[...], mine[...])
    folded = jnp.concatenate([low[quarter:mid], high[quarter:mid]], axis=0)
    gram[:mid, :mid], gram[mid:, mid:] = unfold(folded, low[mid:])
    corner = jnp.concatenate([low[:quarter], high[:quarter]], axis=0)
    gram[mid:, :mid] = corner
    gram[:mid, mid:] = corner.T
    matrix = gram[...]
    row = lax.broadcasted_iota(jnp.int32, matrix.shape, 0)
    column = lax.broadcasted_iota(jnp.int32, matrix.shape, 1)
    eye = (row == column).astype(F32)
    diagonal = matrix * eye
    down = lax.rsqrt(jnp.sum(diagonal, axis=1, keepdims=True))
    along = lax.rsqrt(jnp.sum(diagonal, axis=0, keepdims=True))
    unit = matrix * down * along
    parts = halves(unit)
    a_high[...], a_low[...] = parts

    def correction(error):
        return jnp.where(row > column, error, 0.5 * eye * error).astype(BF16)

    now = (eye - jnp.where(row > column, unit, 0.0)).astype(BF16)
    for _ in range(rounds):
        error = dot(dot(now, a_high[...]).astype(BF16), now, NT) - eye
        exact = now.astype(F32) - dot(correction(error), now)
        now = exact.astype(BF16)
    inverse[...] = exact

    def refined(state):
        full = halves(inverse[...])
        error = dot3(halves(dot3(full, (a_high[...], a_low[...]))), full, NT) - eye
        inverse[...] = inverse[...] - dot(correction(error), full[0])
        return state[0] + 1, jnp.sum(error * error)

    def write_basis(solved):
        basis[...] = (dot3(halves(solved), halves(field[...])) * scale).T

    def write_both():
        solved = inverse[...] * along
        upper = dot3(halves(solved), halves(matrix)) * (1.0 / scale)
        factor[...] = jnp.where(row <= column, upper, 0.0)
        write_basis(solved)

    first = refined((0, 0.0))
    write_both()

    def eliminated():
        inverse[...] = eye
        across = lax.broadcasted_iota(jnp.int32, (1, width), 1)
        down_at = lax.broadcasted_iota(jnp.int32, (width, 1), 0)

        def eliminate(k, _):
            pivot_row = gram[pl.ds(k, 1), :]
            pivot = jnp.sum(jnp.where(across == k, pivot_row, 0.0), axis=1, keepdims=True)
            scaled = pivot_row * lax.rsqrt(pivot)
            now = gram[...]
            below = jnp.sum(jnp.where(column == k, now, 0.0), axis=1, keepdims=True)
            below = jnp.where(down_at > k, below * lax.rsqrt(pivot), 0.0)
            done = inverse[pl.ds(k, 1), :] * lax.rsqrt(pivot)
            factor[pl.ds(k, 1), :] = jnp.where(across >= k, scaled * (1.0 / scale), 0.0)
            gram[...] = now - below * scaled
            inverse[...] = inverse[...] - below * done
            inverse[pl.ds(k, 1), :] = done
            return 0

        lax.fori_loop(0, width, eliminate, 0)
        write_basis(inverse[...])

    @pl.when(jnp.logical_not(first[1] < ENOUGH))
    def _():
        _, left = lax.while_loop(lambda state: (state[0] < REFINED) & (state[1] >= ENOUGH), refined, first)
        pl.when(left < ENOUGH)(write_both)
        pl.when(jnp.logical_not(left < ENOUGH))(eliminated)


def all_reduced(value):
    count = lax.axis_size("tile")
    if count & (count - 1):
        return lax.psum(value, "tile")

    def exchanged(jump):
        return lax.ppermute(value, "tile", [(i, i ^ jump) for i in range(count)])

    bit = 1
    while bit < count:
        if bit == 1 or 2 * bit == count:
            value = value + exchanged(bit)
            bit *= 2
        else:
            first, second, third = exchanged(bit), exchanged(2 * bit), exchanged(3 * bit)
            value = (value + first) + (second + third)
            bit *= 4
    return value


def on_device(jacobian, footprint, live, noise_weight, probes):
    slots, reach, rows, cells = jacobian.shape
    width = probes.shape[2]
    half = slots // lax.axis_size("col")
    cap = slots
    mine = probes[0]

    back, ahead, partner = spread(mine, -2), spread(mine, 2), swapped(mine)
    jac_far = flipped(jacobian)
    staged = kernel_call(
        stage_kernel,
        pltpu.VMEM(jacobian.shape, BF16),
        [HBM],
        VMEM,
        [pltpu.SemaphoreType.DMA(())],
    )(held(jacobian, pltpu.HBM))
    back, staged = lax.optimization_barrier((back, staged))
    table = kernel_call(
        functools.partial(list_kernel, cap, half),
        pltpu.SMEM((len(OFFSETS) * (cap + 1) + reach * slots + 1,), jnp.int32),
        [SMEM] * 2,
        SMEM,
    )(footprint.T, live)
    near = [mine, back, ahead, partner]
    far = [flipped(mine), flipped(back)]
    ahead, partner, _, table = lax.optimization_barrier((ahead, partner, far[1], table))
    table = held(table, pltpu.SMEM)
    far += [flipped(ahead), flipped(partner)]

    early = kernel_call(
        functools.partial(early_kernel, cap),
        (
            jax.ShapeDtypeStruct((half, rows, width), F32),
            jax.ShapeDtypeStruct((half, rows, 2 * cells), BF16),
        ),
        [SMEM] + [VMEM] * 10,
        (VMEM,) * 2,
        [pltpu.VMEM((len(OFFSETS), 2 * cells, width), BF16)],
    )(table, held(staged, pltpu.VMEM), held(jac_far, pltpu.VMEM), *near, *far)
    beyond = swapped(back)
    plain = jax.ShapeDtypeStruct((width, cells), F32)
    message = jax.ShapeDtypeStruct((width + PAD, cells), jnp.int16)
    shares = (held(staged, pltpu.VMEM), held(jac_far, pltpu.VMEM))
    weighted, kept, sent = kernel_call(
        functools.partial(late_kernel, cap),
        (jax.ShapeDtypeStruct((half, width, rows), BF16), plain, message),
        [SMEM] + [VMEM] * 5,
        (VMEM,) * 3,
    )(table, *early, beyond, flipped(beyond), noise_weight)
    kept_ahead, sent_ahead = kernel_call(
        functools.partial(ahead_kernel, cap),
        (plain, message),
        [SMEM] + [VMEM] * 3,
        (VMEM,) * 2,
    )(table, weighted, *shares)

    def merged(value, part):
        return kernel_call(merge_kernel, message, [VMEM] * 2, VMEM)(value, part)

    sent, sent_ahead = lax.optimization_barrier((flipped(sent), sent_ahead))
    beyond = merged(kept, sent)
    beyond, sent_ahead, weighted = lax.optimization_barrier((beyond, sent_ahead, weighted))
    beyond, ahead = swapped(beyond), spread(merged(kept_ahead, flipped(sent_ahead)), -2)
    weighted = kernel_call(
        gather_kernel,
        jax.ShapeDtypeStruct((2 * half + 1, width, rows), BF16),
        [VMEM] * 2,
        VMEM,
    )(weighted, flipped(weighted))

    def buckets(roles, coded, weighted):
        return kernel_call(
            functools.partial(backward_kernel, roles, coded, cap),
            [message if code_it else plain for code_it in coded],
            [SMEM] + [VMEM] * 2,
            [VMEM] * len(roles),
            [pltpu.VMEM((width, cells), F32)],
        )(table, held(staged, pltpu.VMEM), weighted)

    back, partner = buckets(("back", "partner"), (False, True), weighted)
    back = merged(back, beyond)
    back, partner, weighted = lax.optimization_barrier((back, partner, weighted))
    arrived = [spread(back, 2), ahead, swapped(partner)]
    own = buckets(("own",), (False,), weighted)[0]
    packed = jax.ShapeDtypeStruct((width // 2 + ROWS, width // 2), F32)
    field, keep, send = kernel_call(
        field_kernel,
        (plain, packed, packed),
        [VMEM] * 5,
        (VMEM,) * 3,
    )(mine, own, *arrived)
    summed = all_reduced(keep + flipped(send))
    scale = math.sqrt(cells * lax.axis_size("col") * lax.axis_size("tile"))
    square = jax.ShapeDtypeStruct((width, width), F32)
    basis, factor = kernel_call(
        functools.partial(finish_kernel, scale, 2),
        (jax.ShapeDtypeStruct((cells, width), F32), square),
        [VMEM] * 3,
        (VMEM,) * 2,
        [pltpu.VMEM((width, width), F32)] * 2 + [pltpu.VMEM((width, width), BF16)] * 2,
    )(summed, flipped(summed), field)
    return (basis[None], factor)


def solution(mesh):
    placed = (
        P(("groups", "tile"), None, None, "col"),
        P(("groups", "tile"), None),
        P(("groups", "tile")),
        P(("groups", "tile"), None),
        P(("groups", "tile"), "col", None),
    )
    return jax.shard_map(
        on_device,
        mesh=mesh,
        in_specs=placed,
        out_specs=(P(("groups", "tile"), "col", None), P("groups", None)),
        check_vma=False,
    )
```

```python
import functools
import math

import jax
import jax.numpy as jnp
from jax import lax
from jax.experimental import pallas as pl
from jax.experimental.pallas import tpu as pltpu
from jax.sharding import PartitionSpec as P

F32 = jnp.float32
BF16 = jnp.bfloat16
NN = (((1,), (0,)), ((), ()))
NT = (((1,), (1,)), ((), ()))
OFFSETS = (-2, -1, 0, 1, 2)
PAD = 16
ENOUGH = 1e-2
REFINED = 6
ROWS = 8
LIMIT = 16 << 20
VMEM = pl.BlockSpec(memory_space=pltpu.VMEM)
SMEM = pl.BlockSpec(memory_space=pltpu.SMEM)
HBM = pl.BlockSpec(memory_space=pltpu.HBM)
STEP = 4


def kernel_call(body, out_shape, in_specs, out_specs, scratch=(), flops=1024, nbytes=1024):
    return pl.pallas_call(
        body,
        out_shape=out_shape,
        in_specs=in_specs,
        out_specs=out_specs,
        scratch_shapes=list(scratch),
        compiler_params=pltpu.CompilerParams(vmem_limit_bytes=LIMIT),
        cost_estimate=pl.CostEstimate(flops=flops, bytes_accessed=nbytes, transcendentals=0),
    )


def dot(a, b, dims=NN):
    return lax.dot_general(a, b, dims, preferred_element_type=F32)


def halves(a):
    high = a.astype(BF16)
    return high, (a - high.astype(F32)).astype(BF16)


def dot3(a, b, dims=NN):
    a_high, a_low = a
    b_high, b_low = b
    return dot(a_high, b_high, dims) + (dot(a_high, b_low, dims) + dot(a_low, b_high, dims))


held = pltpu.with_memory_space_constraint


def shifted(value, axis, steps):
    count = lax.axis_size(axis)
    pairs = [(source, (source + steps) % count) for source in range(count)]
    return lax.ppermute(value, axis, pairs)


def flipped(value):
    return shifted(value, "col", 1)


def swapped(value):
    return lax.ppermute(value, "tile", [(i, i ^ 1) for i in range(lax.axis_size("tile"))])


def spread(value, steps):
    count = lax.axis_size("tile")
    return lax.ppermute(value, "tile", [(i, (i + (steps, -steps)[i % 2]) % count) for i in range(count)])


ROLES = ("own", "back", "ahead", "partner", "beyond")


def core_index():
    return lax.axis_index("col").astype(jnp.int32)


def place_of(role):
    parity = lax.rem(lax.axis_index("tile").astype(jnp.int32), 2)
    return {
        "own": 2,
        "back": 4 - 4 * parity,
        "ahead": 4 * parity,
        "partner": 3 - 2 * parity,
        "beyond": 1 + 2 * parity,
    }[role]


def list_kernel(cap, half, footprint, live, table):
    reach, slots = footprint.shape
    core = core_index()
    counts = len(OFFSETS) * cap
    places = counts + len(OFFSETS)
    table[places + reach * slots] = live[0]
    for o in range(len(OFFSETS)):
        table[counts + o] = 0

    def step(j, _):
        slot = lax.rem(j + core * half, slots)
        alive = (slot < live[0]).astype(jnp.int32)
        for f in range(reach):
            o = footprint[f, slot]
            table[places + f * slots + slot] = o
            n = table[counts + o]
            table[o * cap + n] = j * 4 + f
            table[counts + o] = n + alive
        return 0

    lax.fori_loop(0, slots, step, 0)


def stage_kernel(value, out, sem):
    copy = pltpu.make_async_copy(value, out, sem)
    copy.start()
    copy.wait()


def early_kernel(cap, table, jac_near, jac_far, *rest):
    count = len(ROLES) - 1
    near, far = rest[:count], rest[count : 2 * count]
    images, aside, window = rest[2 * count :]
    slots = images.shape[0]
    total, reach, _, cells = jac_near.shape
    base = core_index() * slots
    at = len(OFFSETS) * (cap + 1) + base
    for i in range(count):
        o = place_of(ROLES[i])
        window[o, :cells] = near[i][...]
        window[o, cells:] = far[i][...]
    last = place_of(ROLES[count])
    window[last] = jnp.zeros(window.shape[1:], BF16)
    for j in range(slots):
        places = [table[at + f * total + j] for f in range(reach)]
        pieces = [jac[base + j, f] for f in range(reach) for jac in (jac_near, jac_far)]
        bands = [window[place] for place in places]
        images[j] = dot(jnp.concatenate(pieces, axis=1), jnp.concatenate(bands, axis=0))
        chosen = sum(f * (places[f] == last).astype(jnp.int32) for f in range(reach))
        found = sum((place == last).astype(jnp.int32) for place in places)
        for side, jac in enumerate((jac_near, jac_far)):
            block = jac[base + j, chosen]
            aside[j, :, side * cells : (side + 1) * cells] = jnp.where(found > 0, block, jnp.zeros_like(block))


def gather_kernel(mine, other, out):
    half = mine.shape[0]

    def step(j, _):
        out[j] = mine[j]
        out[half + j] = other[j]
        return 0

    lax.fori_loop(0, half, step, 0, unroll=8)
    out[2 * half] = jnp.zeros(out.shape[1:], BF16)


def encode(value, out):
    width = value.shape[0]
    top = jnp.max(jnp.abs(value), axis=0, keepdims=True)
    power = jnp.clip(jnp.floor(jnp.log2(jnp.maximum(top, 1e-30))) + 1.0, -96.0, 96.0)
    coded = jnp.clip(jnp.round(value * jnp.exp2(15.0 - power)), -32767.0, 32767.0)
    out[:width] = coded.astype(jnp.int32).astype(jnp.int16)
    rows = jnp.broadcast_to(power.astype(jnp.int32), (PAD, power.shape[1]))
    out[width:] = rows.astype(jnp.int16)


def decode(part):
    width = part.shape[0] - PAD
    power = part[width:].astype(jnp.int32).astype(F32)[:1]
    return part[:width].astype(jnp.int32).astype(F32) * jnp.exp2(power - 15.0)


def late_kernel(cap, table, images, aside, near, far, noise, out, kept, sent):
    half, width, rows = out.shape
    base = core_index() * half
    live = table[table.shape[0] - 1]
    band = jnp.concatenate([near[...], far[...]], axis=0)
    size = half // 2
    for first in range(0, half, size):
        product = dot(jnp.concatenate([aside[first + j] for j in range(size)], axis=0), band)
        for j in range(size):
            slot = base + first + j
            scale = noise[pl.ds(slot, 1), :] * (slot < live).astype(F32)
            image = images[first + j] + product[j * rows : (j + 1) * rows]
            out[first + j] = (image.T * scale).astype(BF16)

    left = jnp.concatenate([out[j] for j in range(half)], axis=1)
    put_bucket(dot(left, jnp.concatenate([aside[j] for j in range(half)], axis=0)), kept, sent)


def put_bucket(total, kept, sent):
    cells = kept.shape[1]
    kept[...] = total[:, :cells]
    encode(total[:, cells:], sent)


def ahead_kernel(cap, table, weighted, jac_near, jac_far, kept, sent):
    half = weighted.shape[0]
    slots, reach = jac_near.shape[:2]
    base = core_index() * half
    at = len(OFFSETS) * (cap + 1) + base
    wanted = place_of("ahead")
    left, right = [], []
    for j in range(half):
        places = [table[at + f * slots + j] for f in range(reach)]
        chosen = sum(f * (places[f] == wanted).astype(jnp.int32) for f in range(reach))
        found = sum((place == wanted).astype(jnp.int32) for place in places)
        block = weighted[j]
        left.append(jnp.where(found > 0, block, jnp.zeros_like(block)))
        right.append(jnp.concatenate([jac_near[base + j, chosen], jac_far[base + j, chosen]], axis=1))
    put_bucket(dot(jnp.concatenate(left, axis=1), jnp.concatenate(right, axis=0)), kept, sent)


def backward_kernel(roles, coded, cap, table, jac, weighted, *rest):
    outs, total = rest[:-1], rest[-1]
    slots = jac.shape[0]
    half = slots // 2
    counts = len(OFFSETS) * cap
    core = core_index()
    for role, code_it, out in zip(roles, coded, outs, strict=True):
        o = place_of(role)
        count = table[counts + o]

        def product(size):
            left, right = [], []
            for n in range(size):
                code = jnp.where(n < count, table[o * cap + n], slots * 4)
                j, f = lax.shift_right_logical(code, 2), jnp.bitwise_and(code, 3)
                left.append(weighted[j])
                right.append(jac[lax.rem(j + core * half, slots), f])
            total[...] = dot(jnp.concatenate(left, axis=1), jnp.concatenate(right, axis=0))

        below = -1
        for size in range(slots * 3 // 8, slots + 1, STEP):
            pl.when((count > below) & (count <= size))(functools.partial(product, size))
            below = size
        if code_it:
            encode(total[...], out)
        else:
            out[...] = total[...]


def merge_kernel(value, part, out):
    encode(value[...] + decode(part), out)


def field_kernel(probes, own, *rest):
    parts, (field, keep, send) = rest[:3], rest[3:]
    width = own.shape[0]
    total = probes[...].astype(F32).T + own[...]
    for part in parts:
        total = total + decode(part)
    field[...] = total
    both = halves(total)
    gram = dot3(both, both, NT)
    mid, quarter = width // 2, width // 4
    first = core_index() == 0
    corner = gram[mid:, :mid]
    folded, ends = fold(gram[:mid, :mid], gram[mid:, mid:])
    low = jnp.concatenate([corner[:quarter], folded[:quarter], ends], axis=0)
    high = jnp.concatenate([corner[quarter:], folded[quarter:], ends], axis=0)
    keep[...] = jnp.where(first, low, high)
    send[...] = jnp.where(first, high, low)


def positions(square):
    row = lax.broadcasted_iota(jnp.int32, square.shape, 0)
    return row, lax.broadcasted_iota(jnp.int32, square.shape, 1)


def fold(lower, upper):
    row, column = positions(lower)
    diagonal = jnp.sum(jnp.where(row == column, upper, 0.0), axis=0, keepdims=True)
    return jnp.where(row >= column, lower, upper), jnp.broadcast_to(diagonal, (ROWS, lower.shape[1]))


def unfold(folded, ends):
    row, column = positions(folded)
    other = folded.T
    lower = jnp.where(row >= column, folded, other)
    upper = jnp.where(row < column, folded, other)
    return lower, jnp.where(row == column, ends[:1], upper)


def finish_kernel(scale, rounds, mine, other, field, basis, factor, gram, inverse, a_high, a_low):
    width = gram.shape[0]
    mid, quarter = width // 2, width // 4
    first = core_index() == 0
    low = jnp.where(first, mine[...], other[...])
    high = jnp.where(first, other[...], mine[...])
    folded = jnp.concatenate([low[quarter:mid], high[quarter:mid]], axis=0)
    gram[:mid, :mid], gram[mid:, mid:] = unfold(folded, low[mid:])
    corner = jnp.concatenate([low[:quarter], high[:quarter]], axis=0)
    gram[mid:, :mid] = corner
    gram[:mid, mid:] = corner.T
    matrix = gram[...]
    row = lax.broadcasted_iota(jnp.int32, matrix.shape, 0)
    column = lax.broadcasted_iota(jnp.int32, matrix.shape, 1)
    eye = (row == column).astype(F32)
    diagonal = matrix * eye
    down = lax.rsqrt(jnp.sum(diagonal, axis=1, keepdims=True))
    along = lax.rsqrt(jnp.sum(diagonal, axis=0, keepdims=True))
    unit = matrix * down * along
    parts = halves(unit)
    a_high[...], a_low[...] = parts

    def correction(error):
        return jnp.where(row > column, error, 0.5 * eye * error).astype(BF16)

    now = (eye - jnp.where(row > column, unit, 0.0)).astype(BF16)
    for _ in range(rounds):
        error = dot(dot(now, a_high[...]).astype(BF16), now, NT) - eye
        exact = now.astype(F32) - dot(correction(error), now)
        now = exact.astype(BF16)
    inverse[...] = exact

    def refined(state):
        full = halves(inverse[...])
        error = dot3(halves(dot3(full, (a_high[...], a_low[...]))), full, NT) - eye
        inverse[...] = inverse[...] - dot(correction(error), full[0])
        return state[0] + 1, jnp.sum(error * error)

    def write_basis(solved):
        basis[...] = (dot3(halves(solved), halves(field[...])) * scale).T

    def write_both():
        solved = inverse[...] * along
        upper = dot3(halves(solved), halves(matrix)) * (1.0 / scale)
        factor[...] = jnp.where(row <= column, upper, 0.0)
        write_basis(solved)

    first = refined((0, 0.0))
    write_both()

    def eliminated():
        inverse[...] = eye
        across = lax.broadcasted_iota(jnp.int32, (1, width), 1)
        down_at = lax.broadcasted_iota(jnp.int32, (width, 1), 0)

        def eliminate(k, _):
            pivot_row = gram[pl.ds(k, 1), :]
            pivot = jnp.sum(jnp.where(across == k, pivot_row, 0.0), axis=1, keepdims=True)
            scaled = pivot_row * lax.rsqrt(pivot)
            now = gram[...]
            below = jnp.sum(jnp.where(column == k, now, 0.0), axis=1, keepdims=True)
            below = jnp.where(down_at > k, below * lax.rsqrt(pivot), 0.0)
            done = inverse[pl.ds(k, 1), :] * lax.rsqrt(pivot)
            factor[pl.ds(k, 1), :] = jnp.where(across >= k, scaled * (1.0 / scale), 0.0)
            gram[...] = now - below * scaled
            inverse[...] = inverse[...] - below * done
            inverse[pl.ds(k, 1), :] = done
            return 0

        lax.fori_loop(0, width, eliminate, 0)
        write_basis(inverse[...])

    @pl.when(jnp.logical_not(first[1] < ENOUGH))
    def _():
        _, left = lax.while_loop(lambda state: (state[0] < REFINED) & (state[1] >= ENOUGH), refined, first)
        pl.when(left < ENOUGH)(write_both)
        pl.when(jnp.logical_not(left < ENOUGH))(eliminated)


def all_reduced(value):
    count = lax.axis_size("tile")
    if count & (count - 1):
        return lax.psum(value, "tile")

    def exchanged(jump):
        return lax.ppermute(value, "tile", [(i, i ^ jump) for i in range(count)])

    bit = 1
    while bit < count:
        if bit == 1 or 2 * bit == count:
            value = value + exchanged(bit)
            bit *= 2
        else:
            first, second, third = exchanged(bit), exchanged(2 * bit), exchanged(3 * bit)
            value = (value + first) + (second + third)
            bit *= 4
    return value


def on_device(jacobian, footprint, live, noise_weight, probes):
    slots, reach, rows, cells = jacobian.shape
    width = probes.shape[2]
    half = slots // lax.axis_size("col")
    cap = slots
    mine = probes[0]

    back, ahead, partner = spread(mine, -2), spread(mine, 2), swapped(mine)
    jac_far = flipped(jacobian)
    staged = kernel_call(
        stage_kernel,
        pltpu.VMEM(jacobian.shape, BF16),
        [HBM],
        VMEM,
        [pltpu.SemaphoreType.DMA(())],
    )(held(jacobian, pltpu.HBM))
    back, staged = lax.optimization_barrier((back, staged))
    table = kernel_call(
        functools.partial(list_kernel, cap, half),
        pltpu.SMEM((len(OFFSETS) * (cap + 1) + reach * slots + 1,), jnp.int32),
        [SMEM] * 2,
        SMEM,
    )(footprint.T, live)
    near = [mine, back, ahead, partner]
    far = [flipped(mine), flipped(back)]
    ahead, partner, _, table = lax.optimization_barrier((ahead, partner, far[1], table))
    table = held(table, pltpu.SMEM)
    far += [flipped(ahead), flipped(partner)]

    early = kernel_call(
        functools.partial(early_kernel, cap),
        (
            jax.ShapeDtypeStruct((half, rows, width), F32),
            jax.ShapeDtypeStruct((half, rows, 2 * cells), BF16),
        ),
        [SMEM] + [VMEM] * 10,
        (VMEM,) * 2,
        [pltpu.VMEM((len(OFFSETS), 2 * cells, width), BF16)],
    )(table, held(staged, pltpu.VMEM), held(jac_far, pltpu.VMEM), *near, *far)
    beyond = swapped(back)
    plain = jax.ShapeDtypeStruct((width, cells), F32)
    message = jax.ShapeDtypeStruct((width + PAD, cells), jnp.int16)
    shares = (held(staged, pltpu.VMEM), held(jac_far, pltpu.VMEM))
    weighted, kept, sent = kernel_call(
        functools.partial(late_kernel, cap),
        (jax.ShapeDtypeStruct((half, width, rows), BF16), plain, message),
        [SMEM] + [VMEM] * 5,
        (VMEM,) * 3,
    )(table, *early, beyond, flipped(beyond), noise_weight)
    kept_ahead, sent_ahead = kernel_call(
        functools.partial(ahead_kernel, cap),
        (plain, message),
        [SMEM] + [VMEM] * 3,
        (VMEM,) * 2,
    )(table, weighted, *shares)

    def merged(value, part):
        return kernel_call(merge_kernel, message, [VMEM] * 2, VMEM)(value, part)

    sent, sent_ahead = lax.optimization_barrier((flipped(sent), sent_ahead))
    beyond = merged(kept, sent)
    beyond, sent_ahead, weighted = lax.optimization_barrier((beyond, sent_ahead, weighted))
    beyond, ahead = swapped(beyond), spread(merged(kept_ahead, flipped(sent_ahead)), -2)
    weighted = kernel_call(
        gather_kernel,
        jax.ShapeDtypeStruct((2 * half + 1, width, rows), BF16),
        [VMEM] * 2,
        VMEM,
    )(weighted, flipped(weighted))

    def buckets(roles, coded, weighted):
        return kernel_call(
            functools.partial(backward_kernel, roles, coded, cap),
            [message if code_it else plain for code_it in coded],
            [SMEM] + [VMEM] * 2,
            [VMEM] * len(roles),
            [pltpu.VMEM((width, cells), F32)],
        )(table, held(staged, pltpu.VMEM), weighted)

    back, partner = buckets(("back", "partner"), (False, True), weighted)
    back = merged(back, beyond)
    back, partner, weighted = lax.optimization_barrier((back, partner, weighted))
    arrived = [spread(back, 2), ahead, swapped(partner)]
    own = buckets(("own",), (False,), weighted)[0]
    packed = jax.ShapeDtypeStruct((width // 2 + ROWS, width // 2), F32)
    field, keep, send = kernel_call(
        field_kernel,
        (plain, packed, packed),
        [VMEM] * 5,
        (VMEM,) * 3,
    )(mine, own, *arrived)
    summed = all_reduced(keep + flipped(send))
    scale = math.sqrt(cells * lax.axis_size("col") * lax.axis_size("tile"))
    square = jax.ShapeDtypeStruct((width, width), F32)
    basis, factor = kernel_call(
        functools.partial(finish_kernel, scale, 2),
        (jax.ShapeDtypeStruct((cells, width), F32), square),
        [VMEM] * 3,
        (VMEM,) * 2,
        [pltpu.VMEM((width, width), F32)] * 2 + [pltpu.VMEM((width, width), BF16)] * 2,
    )(summed, flipped(summed), field)
    return (basis[None], factor)


def solution(mesh):
    placed = (
        P(("groups", "tile"), None, None, "col"),
        P(("groups", "tile"), None),
        P(("groups", "tile")),
        P(("groups", "tile"), None),
        P(("groups", "tile"), "col", None),
    )
    return jax.shard_map(
        on_device,
        mesh=mesh,
        in_specs=placed,
        out_specs=(P(("groups", "tile"), "col", None), P("groups", None)),
        check_vma=False,
    )
```
